1024 devices in a mesh: dp: 64 (over z, core), expert: 16 (over y, x).
Axes of the slice: x: 4, y: 4, z: 32, core: 2. Of those that a mesh axis runs over, the one named last changes fastest.
Arguments:
- dy_tokens: bfloat16 [32768, 7168], P(('dp', 'expert')), may hold values from -6 to 6
- routing: int32 [32768, 4], P(('dp', 'expert')), may hold values from 0 to 15, all different within a row; in each aligned block of 32 rows (0 to 31, 32 to 63, ...) at most 9 rows name the same one
- route_weight: float32 [32768, 4], P(('dp', 'expert')), may hold values from 0.2 to 2.5
- pre_act: bfloat16 [147456, 256], P(('dp', 'expert')), may hold values from -6 to 6
- gate_weight: bfloat16 [16, 7168, 128], P('expert'), may hold values from -0.0625 to 0.0625
- up_weight: bfloat16 [16, 7168, 128], P('expert'), may hold values from -0.0625 to 0.0625
- down_weight: bfloat16 [16, 128, 7168], P('expert'), may hold values from -0.0625 to 0.0625
Outputs:
- grad_tokens: bfloat16 [32768, 7168], P(('dp', 'expert'))
- grad_down: float32 [16, 128, 7168], P('expert', 'dp')
The draws below stay inside these ranges and needn't reach their ends.
Inputs may be any that keep to these rules, and one draw needn't show every extreme that they name: `routing`: each token names 4 different experts. The tokens of one device name any one expert at most 9 times, and in every draw some device's tokens name some expert exactly 9 times.
All inputs are finite; a program needn't handle non-finite values.
Results may differ from the reference program's by a relative error of at most 0.0064.
Values may be sent and summed in bfloat16 or wider, within the bound.
No kernel may reach another device: no remote copies, remote signals or barrier semaphores. Data moves between devices by JAX's collectives and lax.ppermute only.
A program may use at most 64 MiB of HBM per device.

```python
import math
import jax
import jax.numpy as jnp
import numpy as np
from jax import lax

D = 7168
F_DEV = 128
TOP = 4
TOK_DEV = 32
EXPERTS = 16
CAP = 9
SLOTS = 144
REPLICAS = 64
TOKENS = 32768
DEVICES = 1024


def steps_of(rng, shape, split, smallest, high):
    loudness = 1.0
    for axis_at, shards_of in split:
        draws = jax.random.uniform(jax.random.fold_in(jax.random.fold_in(rng, 6), axis_at), (shards_of,), jnp.float32, smallest / len(split), high / len(split))
        loudness = loudness * jnp.repeat(jnp.exp(draws), shape[axis_at] // shards_of).reshape((-1,) + (1,) * (len(shape) - 1 - axis_at))
    return loudness


def shared_out(own_key, own, number, rows, number_of, top, limit, slope):
    order = jax.random.permutation(own_key, number_of)
    packed, common = portions_of(number_of, rows * top, limit, slope, True), portions_of(number_of, rows * top, limit, slope, False)
    places = jnp.arange(number_of)

    def named(lengths, turn):
        used = int((lengths > 0).sum())
        fixed = max(1, used // 4)
        passed = fixed + (places - fixed + turn * (used - fixed)) % max(1, number_of - fixed)
        return jnp.zeros((number_of,), jnp.int32).at[order[jnp.where(places < fixed, places, passed)]].set(jnp.asarray(lengths, jnp.int32))

    lengths = jnp.where(number % 4 == 0, named(packed, number // 4), named(common, number - number // 4 - 1))
    mixed = jax.random.permutation(jax.random.fold_in(own, 3), number_of)
    source_of, taker = mixed[0:number_of // 2 * 2:2], mixed[1:number_of // 2 * 2:2]
    margin = jnp.minimum(lengths[source_of] - 1, limit - lengths[taker]) // 2
    margin = jnp.where((source_of == order[0]) | (taker == order[0]) | (lengths[taker] == 0), 0, jnp.maximum(margin, 0))
    passed = jax.random.randint(jax.random.fold_in(own, 4), (number_of // 2,), 0, 1 << 20) % (margin + 1)
    lengths = lengths.at[source_of].add(-passed).at[taker].add(passed)
    items = jnp.searchsorted(jnp.cumsum(lengths), jnp.arange(rows * top), side="right").astype(jnp.int32)
    listing = items.reshape(top, rows).T
    listing = listing[jax.random.permutation(jax.random.fold_in(own, 1), rows)]
    turn = jax.random.randint(jax.random.fold_in(own, 2), (rows, 1), 0, top)
    return jnp.take_along_axis(listing, (jnp.arange(top)[None, :] + turn) % top, axis=1)


def portions_of(number_of, total, limit, skew, full):
    portions = [(1 << 20) // math.isqrt(grade ** skew) + 1 for grade in range(1, number_of + 1)]
    largest = limit if full else min(limit, max(-(-total // number_of), total * portions[0] // sum(portions)))
    least = 1 if total - largest >= number_of - 1 else 0
    holding, surplus = [largest] + [least] * (number_of - 1), total - largest - least * (number_of - 1)
    while surplus > 0:
        movable = [i for i in range(1, number_of) if holding[i] < largest] or [i for i in range(1, number_of) if holding[i] < limit]
        whole, budget = sum([portions[i] for i in movable]), surplus
        for i in movable:
            more = min(limit - holding[i], max(1, budget * portions[i] // whole), surplus)
            holding[i] = holding[i] + more
            surplus = surplus - more
    return np.array(holding)


def gaussian(own_key, shape, spread, most, pieces=(), held_as=jnp.bfloat16):
    level = steps_of(own_key, shape, pieces, -0.22, 0.18) if pieces else 1.0
    result = jax.random.normal(own_key, shape, jnp.float32) * spread * level
    return jnp.minimum(jnp.maximum(result, -most), most).astype(held_as)


def setup_inputs(seed: int = 0) -> dict:
    splits = jax.random.split(jax.random.key(seed), 8)
    dy_tokens = gaussian(splits[0], (TOKENS, D), 1.0, 6.0, ((0, 1024),))
    routing_keys = jax.random.split(jax.random.fold_in(splits[1], 1), TOKENS // TOK_DEV)
    routing_turns = jax.random.permutation(jax.random.fold_in(splits[1], 3), TOKENS // TOK_DEV)
    routing = jax.vmap(lambda own, number: shared_out(jax.random.fold_in(splits[1], 2), own, number, TOK_DEV, EXPERTS, TOP, CAP, 1))(routing_keys, routing_turns).reshape((TOKENS, TOP))
    route_weight = jnp.clip(0.2 + 2.3 * jax.random.uniform(splits[2], (TOKENS, TOP), jnp.float32) ** steps_of(splits[2], (TOKENS, TOP), ((0, 1024),), -0.2, 0.2), 0.2, 2.5)
    pre_act = gaussian(splits[3], (DEVICES * SLOTS, 2 * F_DEV), 1.0, 6.0, ((0, 1024),))
    gate_weight = gaussian(splits[4], (EXPERTS, D, F_DEV), D ** -0.5, 0.0625, ((0, 16),))
    up_weight = gaussian(splits[5], (EXPERTS, D, F_DEV), D ** -0.5, 0.0625, ((0, 16),))
    down_weight = gaussian(splits[6], (EXPERTS, F_DEV, D), D ** -0.5, 0.0625, ((0, 16),))
    return dict(dy_tokens=dy_tokens, routing=routing, route_weight=route_weight, pre_act=pre_act, gate_weight=gate_weight, up_weight=up_weight, down_weight=down_weight)


def slot_targets(routing, experts, capacity):
    matches = (routing[:, :, None] == jnp.arange(experts, dtype=jnp.int32)[None, None, :]).astype(jnp.int32)
    per_token = jnp.sum(matches, axis=1)
    before = jnp.cumsum(per_token, axis=0) - per_token
    position = jnp.sum(matches * before[:, None, :], axis=2)
    return (routing * capacity + position).astype(jnp.int32)


def reference(dy_tokens, routing, route_weight, pre_act, gate_weight, up_weight, down_weight):
    dy_split = dy_tokens.reshape(REPLICAS, EXPERTS, TOK_DEV, D)
    route_split = routing.reshape(REPLICAS, EXPERTS, TOK_DEV, TOP)
    weight_split = route_weight.reshape(REPLICAS, EXPERTS, TOK_DEV, TOP)
    pre_split = pre_act.reshape(REPLICAS, EXPERTS, SLOTS, 2 * F_DEV)
    gate_wide = gate_weight.astype(jnp.float32)
    up_wide = up_weight.astype(jnp.float32)
    down_wide = down_weight.astype(jnp.float32)

    def place(slot_index, row_values):
        empty = jnp.zeros((SLOTS, D), jnp.bfloat16)
        return empty.at[slot_index.reshape(-1)].set(row_values.reshape(-1, D))

    def pick(block_rows, slot_index):
        return jnp.take(block_rows, slot_index.reshape(-1), axis=0)

    def replica(running, inputs):
        dy_rep, route_rep, weight_rep, pre_rep = inputs
        targets = jax.vmap(lambda one: slot_targets(one, EXPERTS, CAP))(route_rep)
        scaled = (weight_rep[..., None] * dy_rep[:, :, None, :].astype(jnp.float32)).astype(jnp.bfloat16)
        outgoing = jax.vmap(place)(targets, scaled)
        arrived = outgoing.reshape(EXPERTS, EXPERTS, CAP, D).transpose(1, 0, 2, 3).reshape(EXPERTS, SLOTS, D)
        arrived_wide = arrived.astype(jnp.float32)
        gate_pre = pre_rep[:, :, :F_DEV].astype(jnp.float32)
        up_pre = pre_rep[:, :, F_DEV:].astype(jnp.float32)
        grad_hidden = jnp.einsum('esd,efd->esf', arrived_wide, down_wide)
        sigmoid_gate = jax.nn.sigmoid(gate_pre)
        activated = gate_pre * sigmoid_gate
        hidden = (activated * up_pre).astype(jnp.bfloat16)
        down_term = jnp.einsum('esf,esd->efd', hidden.astype(jnp.float32), arrived_wide)
        grad_up = (grad_hidden * activated).astype(jnp.bfloat16)
        grad_gate = (grad_hidden * up_pre * sigmoid_gate * (1.0 + gate_pre * (1.0 - sigmoid_gate))).astype(jnp.bfloat16)
        grad_rows = jnp.einsum('esf,edf->esd', grad_gate.astype(jnp.float32), gate_wide)
        grad_rows = grad_rows + jnp.einsum('esf,edf->esd', grad_up.astype(jnp.float32), up_wide)
        grad_rows = grad_rows.astype(jnp.bfloat16)
        returned = grad_rows.reshape(EXPERTS, EXPERTS, CAP, D).transpose(1, 0, 2, 3).reshape(EXPERTS, SLOTS, D)
        picked = jax.vmap(pick)(returned, targets)
        token_grads = jnp.sum(picked.reshape(EXPERTS, TOK_DEV, TOP, D).astype(jnp.float32), axis=2).astype(jnp.bfloat16)
        return running + down_term, token_grads

    start_total = jnp.zeros((EXPERTS, F_DEV, D), jnp.float32)
    grad_total, token_grads = lax.scan(replica, start_total, (dy_split, route_split, weight_split, pre_split))
    grad_down = grad_total / REPLICAS
    return token_grads.reshape(TOKENS, D), grad_down
```

```python
import functools

import jax
import jax.numpy as jnp
from jax import lax
from jax.experimental import pallas as pl
from jax.experimental.pallas import tpu as pltpu
from jax.sharding import PartitionSpec as P

BF = jnp.bfloat16
F32 = jnp.float32
LANES = 128
FIRST = 8
PARAMS = pltpu.CompilerParams(vmem_limit_bytes=40 * 1024 * 1024)


def dot(a, b, contract):
    return lax.dot_general(a, b, (contract, ((), ())), preferred_element_type=F32)


def iota(shape, axis):
    return lax.broadcasted_iota(jnp.int32, shape, axis)


def write_block(ref, tail, pair, first, second, experts):
    main = experts * FIRST
    tiles = [x[:main].reshape(experts, FIRST, LANES) for x in (first, second)]
    ref[:, pair * 16 : pair * 16 + 16, :] = jnp.concatenate(tiles, axis=1).astype(BF)
    tail[:, 2 * pair, :] = first[main:]
    tail[:, 2 * pair + 1, :] = second[main:]


def read_block(ref, tail, pair, experts):
    both = ref[:, pair * 16 : pair * 16 + 16, :].astype(F32)
    main = experts * FIRST
    halves = []
    for at in range(2):
        block = both[:, at * FIRST : (at + 1) * FIRST, :].reshape(main, LANES)
        halves.append(jnp.concatenate([block, tail[:, 2 * pair + at, :]], axis=0))
    return jnp.concatenate(halves, axis=1)


def dispatch_kernel(experts, dy_ref, routing_ref, weight_ref, out_ref, pick_ref, tail):
    tokens, width = dy_ref.shape
    route_count = routing_ref.shape[1]
    main = experts * FIRST
    lanes = pick_ref.shape[1]
    slot = iota((tokens, lanes), 1)
    expert = jnp.where(slot < main, slot // FIRST, slot - main)
    position = jnp.where(slot < main, slot % FIRST, FIRST)
    named = jnp.zeros((tokens, lanes), F32)
    scale = jnp.zeros((tokens, lanes), F32)
    for k in range(route_count):
        hit = routing_ref[:, k : k + 1] == expert
        named = named + jnp.where(hit, 1.0, 0.0)
        scale = scale + jnp.where(hit, weight_ref[:, k : k + 1], 0.0)
    earlier = jnp.where(iota((tokens, tokens), 1) < iota((tokens, tokens), 0), 1.0, 0.0)
    before = dot(earlier.astype(BF), named.astype(BF), ((1,), (0,)))
    pick = jnp.where((named > 0.5) & (before == position.astype(F32)), 1.0, 0.0)
    pick_ref[...] = pick.astype(BF)
    rows = main + experts
    chosen = pick[:, :rows].astype(BF)
    rest = (pick * scale)[:, :rows]
    ones = jnp.ones((tokens, LANES), BF)
    row_weight = jnp.zeros((rows, LANES), F32)
    for _ in range(3):
        piece = rest.astype(BF)
        row_weight = row_weight + dot(piece, ones, ((0,), (0,)))
        rest = rest - piece.astype(F32)
    row_weight = jnp.concatenate([row_weight, row_weight], axis=1)
    for pair in range(width // (2 * LANES)):
        part = dot(chosen, dy_ref[:, pair * 2 * LANES : (pair + 1) * 2 * LANES], ((0,), (0,)))
        part = part * row_weight
        write_block(out_ref, tail, pair, part[:, :LANES], part[:, LANES:], experts)
    out_ref[:, experts_rows(width) :, :] = tail[...].astype(BF)


def experts_rows(width):
    return width // LANES * FIRST


def partial_kernel(
    experts, z_lo, own_ref, got_ref, pre_ref, arrived_ref, keep_ref, send_ref, factor_ref, tail
):
    rows, width = arrived_ref.shape
    hidden_units = pre_ref.shape[1] // 2
    main = experts * FIRST
    capacity = rows // experts
    new, old = iota((rows, rows), 0), iota((rows, rows), 1)
    source = jnp.where(
        new < main, new // FIRST * capacity + new % FIRST, (new - main) * capacity + FIRST
    )
    order = jnp.where(source == old, 1.0, 0.0).astype(BF)
    pre = dot(order, pre_ref[...], ((1,), (0,)))
    gate_pre, up_pre = pre[:, :hidden_units], pre[:, hidden_units:]
    sigmoid = 1.0 / (1.0 + jnp.exp(-gate_pre))
    activated = gate_pre * sigmoid
    factor_ref[:, :hidden_units] = up_pre * sigmoid * (1.0 + gate_pre * (1.0 - sigmoid))
    factor_ref[:, hidden_units:] = activated
    hidden = (activated * up_pre).astype(BF)
    half = hidden_units // 2
    block = half // z_lo
    unit, at = iota((hidden_units, hidden_units), 0), iota((hidden_units, hidden_units), 1)
    core = jnp.where(at < half, own_ref[0], 1 - own_ref[0])
    r = at % half
    target = 4 * (z_lo * ((r % block) // 2) + r // block) + 2 * core + r % 2
    hidden = dot(hidden, jnp.where(unit == target, 1.0, 0.0).astype(BF), ((1,), (0,))).astype(BF)
    tail[...] = got_ref[:, experts_rows(width) :, :].astype(F32)
    for pair in range(width // (2 * LANES)):
        at = slice(pair * 2 * LANES, (pair + 1) * 2 * LANES)
        arrived = read_block(got_ref, tail, pair, experts).astype(BF)
        arrived_ref[:, at] = arrived
        part = dot(hidden, arrived, ((0,), (0,)))
        keep_ref[:, at] = part[:half]
        send_ref[:, at] = part[half:].astype(BF)


def grad_kernel(experts, arrived_ref, factor_ref, gate_ref, up_ref, down_ref, out_ref, tail):
    width = arrived_ref.shape[1]
    hidden_units = down_ref.shape[1]
    grad_hidden = dot(arrived_ref[...], down_ref[0], ((1,), (1,)))
    grad_gate = (grad_hidden * factor_ref[:, :hidden_units]).astype(BF)
    grad_up = (grad_hidden * factor_ref[:, hidden_units:]).astype(BF)
    for pair in range(width // (2 * LANES)):
        at = slice(pair * 2 * LANES, (pair + 1) * 2 * LANES)
        part = dot(grad_gate, gate_ref[0, at, :], ((1,), (1,)))
        part = part + dot(grad_up, up_ref[0, at, :], ((1,), (1,)))
        write_block(out_ref, tail, pair, part[:, :LANES], part[:, LANES:], experts)
    out_ref[:, experts_rows(width) :, :] = tail[...].astype(BF)


def combine_kernel(experts, pick_ref, got_ref, out_ref, tail):
    width = out_ref.shape[1]
    tail[...] = got_ref[:, experts_rows(width) :, :].astype(F32)
    pick = pick_ref[:, : experts * (FIRST + 1)]
    for pair in range(width // (2 * LANES)):
        rows = read_block(got_ref, tail, pair, experts).astype(BF)
        out_ref[:, pair * 2 * LANES : (pair + 1) * 2 * LANES] = dot(
            pick, rows, ((1,), (0,))
        ).astype(BF)


def per_device(dy_tokens, routing, route_weight, pre_act, gate_weight, up_weight, down_weight):
    experts = lax.axis_size("expert")
    replicas = lax.axis_size("dp")
    tokens, width = dy_tokens.shape
    rows = pre_act.shape[0]
    hidden_units = down_weight.shape[1]
    capacity = rows // experts
    assert capacity == FIRST + 1
    block_rows = capacity * width // LANES
    chips = replicas // 2
    z_lo = 4
    z_hi = chips // z_lo
    shape = jax.ShapeDtypeStruct
    vmem = pl.BlockSpec(memory_space=pltpu.VMEM)
    smem = pl.BlockSpec(memory_space=pltpu.SMEM)
    tail = pltpu.VMEM((experts, width // LANES, LANES), F32)
    block = shape((experts, block_rows, LANES), BF)

    outgoing, pick = pl.pallas_call(
        functools.partial(dispatch_kernel, experts),
        out_shape=(block, shape((tokens, 2 * LANES), BF)),
        in_specs=[vmem] * 3,
        out_specs=(vmem, vmem),
        scratch_shapes=[tail],
        compiler_params=PARAMS,
        name="dispatch_rows",
    )(dy_tokens, routing, route_weight)
    got = lax.all_to_all(outgoing, "expert", split_axis=0, concat_axis=0, tiled=True)

    core = lax.axis_index("dp") % 2
    half = hidden_units // 2
    arrived, keep, send, factor = pl.pallas_call(
        functools.partial(partial_kernel, experts, z_lo),
        out_shape=(
            shape((rows, width), BF),
            shape((half, width), F32),
            shape((half, width), BF),
            shape((rows, 2 * hidden_units), F32),
        ),
        in_specs=[smem, vmem, vmem],
        out_specs=(vmem,) * 4,
        scratch_shapes=[tail],
        compiler_params=PARAMS,
        name="down_partial",
    )(core.reshape(1), got, pre_act)
    other = lax.ppermute(send, "dp", [(i, i ^ 1) for i in range(replicas)])

    going_back = pl.pallas_call(
        functools.partial(grad_kernel, experts),
        out_shape=block,
        in_specs=[vmem] * 5,
        out_specs=vmem,
        scratch_shapes=[tail],
        compiler_params=PARAMS,
        name="grad_rows",
    )(arrived, factor, gate_weight, up_weight, down_weight)
    returned = lax.all_to_all(going_back, "expert", split_axis=0, concat_axis=0, tiled=True)

    near = [
        [2 * (z_lo * g + i) + c for i in range(z_lo)] for g in range(z_hi) for c in range(2)
    ]
    far = [[2 * (z_lo * i + g) + c for i in range(z_hi)] for g in range(z_lo) for c in range(2)]
    paired = (keep + other.astype(F32)).astype(BF).reshape(z_lo, half // z_lo, width)
    paired = lax.all_to_all(paired, "dp", 0, 0, axis_index_groups=near, tiled=True)
    summed = jnp.sum(paired.astype(F32), axis=0).astype(BF)
    summed = summed.reshape(z_hi, 2 * width // LANES, LANES)
    summed = lax.all_to_all(summed, "dp", 0, 0, axis_index_groups=far, tiled=True)
    grad_down = (jnp.sum(summed.astype(F32), axis=0) * (1.0 / replicas)).reshape(1, 2, width)

    grad_tokens = pl.pallas_call(
        functools.partial(combine_kernel, experts),
        out_shape=shape((tokens, width), BF),
        in_specs=[vmem] * 2,
        out_specs=vmem,
        scratch_shapes=[tail],
        compiler_params=PARAMS,
        name="combine_rows",
    )(pick, returned)
    return (grad_tokens, grad_down)


def solution(mesh):
    placed = (
        P(("dp", "expert"), None),
        P(("dp", "expert"), None),
        P(("dp", "expert"), None),
        P(("dp", "expert"), None),
        P("expert", None, None),
        P("expert", None, None),
        P("expert", None, None),
    )
    return jax.shard_map(
        per_device,
        mesh=mesh,
        in_specs=placed,
        out_specs=(P(("dp", "expert"), None), P("expert", "dp", None)),
        check_vma=False,
    )
```

```python
import functools

import jax
import jax.numpy as jnp
from jax import lax
from jax.experimental import pallas as pl
from jax.experimental.pallas import tpu as pltpu
from jax.sharding import PartitionSpec as P

BF = jnp.bfloat16
F32 = jnp.float32
LANES = 128
FIRST = 8
PARAMS = pltpu.CompilerParams(vmem_limit_bytes=16 * 1024 * 1024)


def dot(a, b, contract):
    return lax.dot_general(a, b, (contract, ((), ())), preferred_element_type=F32)


def iota(shape, axis):
    return lax.broadcasted_iota(jnp.int32, shape, axis)


def write_block(ref, tail, pair, first, second, experts):
    main = experts * FIRST
    tiles = [x[:main].reshape(experts, FIRST, LANES) for x in (first, second)]
    ref[:, pair * 16 : pair * 16 + 16, :] = jnp.concatenate(tiles, axis=1).astype(BF)
    tail[:, 2 * pair, :] = first[main:]
    tail[:, 2 * pair + 1, :] = second[main:]


def read_block(ref, tail, pair, experts):
    both = ref[:, pair * 16 : pair * 16 + 16, :].astype(F32)
    main = experts * FIRST
    halves = []
    for at in range(2):
        block = both[:, at * FIRST : (at + 1) * FIRST, :].reshape(main, LANES)
        halves.append(jnp.concatenate([block, tail[:, 2 * pair + at, :]], axis=0))
    return jnp.concatenate(halves, axis=1)


def dispatch_kernel(
    experts, dy_hbm, routing_hbm, weight_hbm, out_hbm, pick_ref, dy_ref, routing_ref, weight_ref, out_ref, tail, sems
):
    loads = [
        pltpu.make_async_copy(source, target, sems.at[i])
        for i, (source, target) in enumerate(
            [(routing_hbm, routing_ref), (weight_hbm, weight_ref), (dy_hbm, dy_ref)]
        )
    ]
    for load in loads:
        load.start()
    loads[0].wait()
    loads[1].wait()
    tokens, width = dy_ref.shape
    route_count = routing_ref.shape[0]
    main = experts * FIRST
    rows = main + experts
    slot = iota((rows, tokens), 0)
    expert = jnp.where(slot < main, slot // FIRST, slot - main)
    position = jnp.where(slot < main, slot % FIRST, FIRST)
    named = jnp.zeros((rows, tokens), F32)
    scale = jnp.zeros((rows, tokens), F32)
    for k in range(route_count):
        hit = routing_ref[k : k + 1, :] == expert
        named = named + jnp.where(hit, 1.0, 0.0)
        scale = scale + jnp.where(hit, weight_ref[k : k + 1, :], 0.0)
    earlier = jnp.where(iota((tokens, tokens), 0) < iota((tokens, tokens), 1), 1.0, 0.0)
    before = dot(named.astype(BF), earlier.astype(BF), ((1,), (0,)))
    pick = jnp.where((named > 0.5) & (before == position.astype(F32)), 1.0, 0.0)
    chosen = pick.astype(BF)
    pick_ref[...] = chosen
    row_weight = jnp.sum(pick * scale, axis=1, keepdims=True)
    pairs = width // (2 * LANES)
    parts = 4
    stores = []
    loads[2].wait()
    for pair in range(pairs):
        part = dot(chosen, dy_ref[:, pair * 2 * LANES : (pair + 1) * 2 * LANES], ((1,), (0,)))
        part = part * row_weight
        write_block(out_ref, tail, pair, part[:, :LANES], part[:, LANES:], experts)
        if (pair + 1) % (pairs // parts) == 0:
            rows_of = slice(len(stores) * pairs // parts * 16, (pair + 1) * 16)
            if pair + 1 == pairs:
                out_ref[:, experts_rows(width) :, :] = tail[...].astype(BF)
                rows_of = slice(rows_of.start, out_ref.shape[1])
            stores.append(
                pltpu.make_async_copy(
                    out_ref.at[:, rows_of, :], out_hbm.at[:, rows_of, :], sems.at[3 + len(stores)]
                )
            )
            stores[-1].start()
    for store in stores:
        store.wait()


def experts_rows(width):
    return width // LANES * FIRST


def partial_kernel(
    experts, chips, at_ref, got_ref, pre_ref, arrived_ref, keep_ref, send_ref, factor_ref, tail
):
    rows, width = arrived_ref.shape
    hidden_units = pre_ref.shape[1] // 2
    main = experts * FIRST
    capacity = rows // experts
    new, old = iota((rows, rows), 0), iota((rows, rows), 1)
    source = jnp.where(
        new < main, new // FIRST * capacity + new % FIRST, (new - main) * capacity + FIRST
    )
    order = jnp.where(source == old, 1.0, 0.0).astype(BF)
    pre = dot(order, pre_ref[...], ((1,), (0,)))
    gate_pre, up_pre = pre[:, :hidden_units], pre[:, hidden_units:]
    sigmoid = 1.0 / (1.0 + jnp.exp(-gate_pre))
    activated = gate_pre * sigmoid
    factor_ref[:, :hidden_units] = up_pre * sigmoid * (1.0 + gate_pre * (1.0 - sigmoid))
    factor_ref[:, hidden_units:] = activated
    hidden = (activated * up_pre).astype(BF)
    half = hidden_units // 2
    unit, at = iota((hidden_units, hidden_units), 0), iota((hidden_units, hidden_units), 1)
    core = jnp.where(at < half, at_ref[1], 1 - at_ref[1])
    share = half // chips
    place = at % half // share
    far = jnp.zeros_like(place)
    bits = chips.bit_length() - 1
    for bit in range(bits):
        far = far + (place // 2**bit) % 2 * 2 ** (bits - 1 - bit)
    chip = (at_ref[0] + (1 - 2 * core) * far + chips) % chips
    target = (2 * chip + core) * share + at % share
    hidden = dot(hidden, jnp.where(unit == target, 1.0, 0.0).astype(BF), ((1,), (0,))).astype(BF)
    tail[...] = got_ref[:, experts_rows(width) :, :].astype(F32)
    for pair in range(width // (2 * LANES)):
        at = slice(pair * 2 * LANES, (pair + 1) * 2 * LANES)
        arrived = read_block(got_ref, tail, pair, experts).astype(BF)
        arrived_ref[:, at] = arrived
        part = dot(hidden, arrived, ((0,), (0,)))
        keep_ref[:, at] = part[:half]
        send_ref[:, at] = part[half:].astype(BF)


def grad_kernel(experts, arrived_ref, factor_ref, gate_ref, up_ref, down_ref, out_ref, tail):
    width = arrived_ref.shape[1]
    hidden_units = down_ref.shape[1]
    grad_hidden = dot(arrived_ref[...], down_ref[0], ((1,), (1,)))
    grad_gate = (grad_hidden * factor_ref[:, :hidden_units]).astype(BF)
    grad_up = (grad_hidden * factor_ref[:, hidden_units:]).astype(BF)
    for pair in range(width // (2 * LANES)):
        at = slice(pair * 2 * LANES, (pair + 1) * 2 * LANES)
        part = dot(grad_gate, gate_ref[0, at, :], ((1,), (1,)))
        part = part + dot(grad_up, up_ref[0, at, :], ((1,), (1,)))
        write_block(out_ref, tail, pair, part[:, :LANES], part[:, LANES:], experts)
    out_ref[:, experts_rows(width) :, :] = tail[...].astype(BF)


def combine_kernel(experts, pick_ref, got_ref, out_ref, tail):
    width = out_ref.shape[1]
    tail[...] = got_ref[:, experts_rows(width) :, :].astype(F32)
    pick = pick_ref[...]
    for pair in range(width // (2 * LANES)):
        rows = read_block(got_ref, tail, pair, experts).astype(BF)
        out_ref[:, pair * 2 * LANES : (pair + 1) * 2 * LANES] = dot(
            pick, rows, ((0,), (0,))
        ).astype(BF)


def per_device(dy_tokens, routing, route_weight, pre_act, gate_weight, up_weight, down_weight):
    experts = lax.axis_size("expert")
    replicas = lax.axis_size("dp")
    tokens, width = dy_tokens.shape
    rows = pre_act.shape[0]
    hidden_units = down_weight.shape[1]
    capacity = rows // experts
    assert capacity == FIRST + 1
    block_rows = capacity * width // LANES
    chips = replicas // 2
    assert chips & (chips - 1) == 0 and hidden_units % replicas == 0
    shape = jax.ShapeDtypeStruct
    vmem = pl.BlockSpec(memory_space=pltpu.VMEM)
    smem = pl.BlockSpec(memory_space=pltpu.SMEM)
    tail = pltpu.VMEM((experts, width // LANES, LANES), F32)
    block = shape((experts, block_rows, LANES), BF)

    outgoing, pick = pl.pallas_call(
        functools.partial(dispatch_kernel, experts),
        out_shape=(pltpu.HBM(block.shape, BF), shape((rows, tokens), BF)),
        in_specs=[pl.BlockSpec(memory_space=pl.ANY)] * 3,
        out_specs=(pl.BlockSpec(memory_space=pltpu.HBM), vmem),
        scratch_shapes=[
            pltpu.VMEM((tokens, width), BF),
            pltpu.VMEM(routing.T.shape, jnp.int32),
            pltpu.VMEM(route_weight.T.shape, F32),
            pltpu.VMEM((experts, block_rows, LANES), BF),
            tail,
            pltpu.SemaphoreType.DMA((7,)),
        ],
        compiler_params=PARAMS,
        name="dispatch_rows",
    )(*(pltpu.with_memory_space_constraint(x, pltpu.HBM) for x in (dy_tokens, routing.T, route_weight.T)))
    got = lax.all_to_all(outgoing, "expert", split_axis=0, concat_axis=0, tiled=True)

    own = lax.axis_index("dp")
    half = hidden_units // 2
    arrived, keep, send, factor = pl.pallas_call(
        functools.partial(partial_kernel, experts, chips),
        out_shape=(
            shape((rows, width), BF),
            shape((half, width), F32),
            shape((half, width), BF),
            shape((rows, 2 * hidden_units), F32),
        ),
        in_specs=[smem, vmem, vmem],
        out_specs=(vmem,) * 4,
        scratch_shapes=[tail],
        compiler_params=PARAMS,
        name="down_partial",
    )(jnp.stack([own // 2, own % 2]), got, pre_act)
    other = lax.ppermute(send, "dp", [(i, i ^ 1) for i in range(replicas)])

    going_back = pl.pallas_call(
        functools.partial(grad_kernel, experts),
        out_shape=block,
        in_specs=[vmem] * 5,
        out_specs=vmem,
        scratch_shapes=[tail],
        compiler_params=PARAMS,
        name="grad_rows",
    )(arrived, factor, gate_weight, up_weight, down_weight)
    returned = lax.all_to_all(going_back, "expert", split_axis=0, concat_axis=0, tiled=True)

    grad_tokens = pl.pallas_call(
        functools.partial(combine_kernel, experts),
        out_shape=shape((tokens, width), BF),
        in_specs=[vmem] * 2,
        out_specs=vmem,
        scratch_shapes=[tail],
        compiler_params=PARAMS,
        name="combine_rows",
    )(pick, returned)
    terms, count, distance = [keep, other], half, 1
    while distance < chips:
        count //= 2
        going = functools.reduce(jnp.add, [t[count:].astype(F32) for t in terms]).astype(BF)
        if 2 * distance == chips:
            going, grad_tokens = lax.optimization_barrier((going, grad_tokens))
        hops = [
            (2 * z + c, 2 * ((z + (distance if c == 0 else -distance)) % chips) + c)
            for z in range(chips)
            for c in range(2)
        ]
        coming = lax.ppermute(going, "dp", hops)
        terms = [t[:count] for t in terms] + [coming]
        distance *= 2
    grad_down = functools.reduce(jnp.add, [t.astype(F32) for t in terms]) * (1.0 / replicas)
    grad_down = grad_down[None]

    return (grad_tokens, grad_down)


def solution(mesh):
    placed = (
        P(("dp", "expert"), None),
        P(("dp", "expert"), None),
        P(("dp", "expert"), None),
        P(("dp", "expert"), None),
        P("expert", None, None),
        P("expert", None, None),
        P("expert", None, None),
    )
    return jax.shard_map(
        per_device,
        mesh=mesh,
        in_specs=placed,
        out_specs=(P(("dp", "expert"), None), P("expert", "dp", None)),
        check_vma=False,
    )
```

```python
import functools

import jax
import jax.numpy as jnp
from jax import lax
from jax.experimental import pallas as pl
from jax.experimental.pallas import tpu as pltpu
from jax.sharding import PartitionSpec as P

BF = jnp.bfloat16
F32 = jnp.float32
LANES = 128
FIRST = 8
PARAMS = pltpu.CompilerParams(vmem_limit_bytes=16 * 1024 * 1024)


def dot(a, b, contract):
    return lax.dot_general(a, b, (contract, ((), ())), preferred_element_type=F32)


def iota(shape, axis):
    return lax.broadcasted_iota(jnp.int32, shape, axis)


def write_block(ref, tail, pair, first, second, experts):
    main = experts * FIRST
    tiles = [x[:main].reshape(experts, FIRST, LANES) for x in (first, second)]
    ref[:, pair * 16 : pair * 16 + 16, :] = jnp.concatenate(tiles, axis=1).astype(BF)
    tail[:, 2 * pair, :] = first[main:]
    tail[:, 2 * pair + 1, :] = second[main:]


def read_block(ref, tail, pair, experts):
    both = ref[:, pair * 16 : pair * 16 + 16, :].astype(F32)
    main = experts * FIRST
    halves = []
    for at in range(2):
        block = both[:, at * FIRST : (at + 1) * FIRST, :].reshape(main, LANES)
        halves.append(jnp.concatenate([block, tail[:, 2 * pair + at, :]], axis=0))
    return jnp.concatenate(halves, axis=1)


def dispatch_kernel(
    experts, dy_hbm, routing_hbm, weight_hbm, out_hbm, pick_ref, dy_ref, routing_ref, weight_ref, out_ref, tail, sems
):
    loads = [
        pltpu.make_async_copy(source, target, sems.at[i])
        for i, (source, target) in enumerate(
            [(routing_hbm, routing_ref), (weight_hbm, weight_ref), (dy_hbm, dy_ref)]
        )
    ]
    for load in loads:
        load.start()
    loads[0].wait()
    loads[1].wait()
    tokens, width = dy_ref.shape
    route_count = routing_ref.shape[0]
    main = experts * FIRST
    rows = main + experts
    slot = iota((rows, tokens), 0)
    expert = jnp.where(slot < main, slot // FIRST, slot - main)
    position = jnp.where(slot < main, slot % FIRST, FIRST)
    named = jnp.zeros((rows, tokens), F32)
    scale = jnp.zeros((rows, tokens), F32)
    for k in range(route_count):
        hit = routing_ref[k : k + 1, :] == expert
        named = named + jnp.where(hit, 1.0, 0.0)
        scale = scale + jnp.where(hit, weight_ref[k : k + 1, :], 0.0)
    earlier = jnp.where(iota((tokens, tokens), 0) < iota((tokens, tokens), 1), 1.0, 0.0)
    before = dot(named.astype(BF), earlier.astype(BF), ((1,), (0,)))
    pick = jnp.where((named > 0.5) & (before == position.astype(F32)), 1.0, 0.0)
    chosen = pick.astype(BF)
    pick_ref[...] = chosen
    row_weight = jnp.sum(pick * scale, axis=1, keepdims=True)
    pairs = width // (2 * LANES)
    parts = 4
    stores = []
    loads[2].wait()
    for pair in range(pairs):
        part = dot(chosen, dy_ref[:, pair * 2 * LANES : (pair + 1) * 2 * LANES], ((1,), (0,)))
        part = part * row_weight
        write_block(out_ref, tail, pair, part[:, :LANES], part[:, LANES:], experts)
        if (pair + 1) % (pairs // parts) == 0:
            rows_of = slice(len(stores) * pairs // parts * 16, (pair + 1) * 16)
            if pair + 1 == pairs:
                out_ref[:, experts_rows(width) :, :] = tail[...].astype(BF)
                rows_of = slice(rows_of.start, out_ref.shape[1])
            stores.append(
                pltpu.make_async_copy(
                    out_ref.at[:, rows_of, :], out_hbm.at[:, rows_of, :], sems.at[3 + len(stores)]
                )
            )
            stores[-1].start()
    for store in stores:
        store.wait()


def experts_rows(width):
    return width // LANES * FIRST


def partial_kernel(
    experts, chips, groups, at_ref, got_ref, pre_ref, arrived_ref, keep_ref, send_ref, factor_ref, tail
):
    rows, width = arrived_ref.shape
    hidden_units = pre_ref.shape[1] // 2
    main = experts * FIRST
    capacity = rows // experts
    new, old = iota((rows, rows), 0), iota((rows, rows), 1)
    source = jnp.where(
        new < main, new // FIRST * capacity + new % FIRST, (new - main) * capacity + FIRST
    )
    order = jnp.where(source == old, 1.0, 0.0).astype(BF)
    pre = dot(order, pre_ref[...], ((1,), (0,)))
    gate_pre, up_pre = pre[:, :hidden_units], pre[:, hidden_units:]
    sigmoid = 1.0 / (1.0 + jnp.exp(-gate_pre))
    activated = gate_pre * sigmoid
    factor_ref[:, :hidden_units] = up_pre * sigmoid * (1.0 + gate_pre * (1.0 - sigmoid))
    factor_ref[:, hidden_units:] = activated
    hidden = (activated * up_pre).astype(BF)
    half = hidden_units // 2
    unit, at = iota((hidden_units, hidden_units), 0), iota((hidden_units, hidden_units), 1)
    core = jnp.where(at < half, at_ref[1], 1 - at_ref[1])
    share = half // chips
    place = at % half // share
    ahead = place // groups
    far = jnp.zeros_like(place)
    bits = (chips // groups).bit_length() - 1
    for bit in range(bits):
        far = far + (ahead // 2**bit) % 2 * 2 ** (bits - 1 - bit)
    period = chips // groups
    chip = place % groups * period + (at_ref[0] + (1 - 2 * core) * far + chips) % period
    target = (2 * chip + core) * share + at % share
    hidden = dot(hidden, jnp.where(unit == target, 1.0, 0.0).astype(BF), ((1,), (0,))).astype(BF)
    tail[...] = got_ref[:, experts_rows(width) :, :].astype(F32)
    for pair in range(width // (2 * LANES)):
        at = slice(pair * 2 * LANES, (pair + 1) * 2 * LANES)
        arrived = read_block(got_ref, tail, pair, experts).astype(BF)
        arrived_ref[:, at] = arrived
        part = dot(hidden, arrived, ((0,), (0,)))
        keep_ref[:, at] = part[:half]
        send_ref[:, at] = part[half:].astype(BF)


def grad_kernel(experts, arrived_ref, factor_ref, gate_ref, up_ref, down_ref, out_ref, tail):
    width = arrived_ref.shape[1]
    hidden_units = down_ref.shape[1]
    grad_hidden = dot(arrived_ref[...], down_ref[0], ((1,), (1,)))
    grad_gate = (grad_hidden * factor_ref[:, :hidden_units]).astype(BF)
    grad_up = (grad_hidden * factor_ref[:, hidden_units:]).astype(BF)
    for pair in range(width // (2 * LANES)):
        at = slice(pair * 2 * LANES, (pair + 1) * 2 * LANES)
        part = dot(grad_gate, gate_ref[0, at, :], ((1,), (1,)))
        part = part + dot(grad_up, up_ref[0, at, :], ((1,), (1,)))
        write_block(out_ref, tail, pair, part[:, :LANES], part[:, LANES:], experts)
    out_ref[:, experts_rows(width) :, :] = tail[...].astype(BF)


def combine_kernel(experts, pick_ref, got_ref, out_ref, tail):
    width = out_ref.shape[1]
    tail[...] = got_ref[:, experts_rows(width) :, :].astype(F32)
    pick = pick_ref[...]
    for pair in range(width // (2 * LANES)):
        rows = read_block(got_ref, tail, pair, experts).astype(BF)
        out_ref[:, pair * 2 * LANES : (pair + 1) * 2 * LANES] = dot(
            pick, rows, ((0,), (0,))
        ).astype(BF)


def fold_kernel(total_ref, coming_ref, out_ref, lines):
    for c in range(lines.shape[1]):
        at = slice(c * LANES, (c + 1) * LANES)
        lines[:, c, :] = total_ref[:, at] + coming_ref[:, at].astype(F32)
    out_ref[...] = lines[...].reshape(out_ref.shape).astype(BF)


def finish_kernel(scale, coming_ref, out_ref, lines):
    total = coming_ref[0].astype(F32)
    for g in range(1, coming_ref.shape[0]):
        total = total + coming_ref[g].astype(F32)
    lines[...] = (total * scale).reshape(lines.shape)
    for c in range(lines.shape[1]):
        out_ref[0, :, c * LANES : (c + 1) * LANES] = lines[:, c, :]


def per_device(dy_tokens, routing, route_weight, pre_act, gate_weight, up_weight, down_weight):
    experts = lax.axis_size("expert")
    replicas = lax.axis_size("dp")
    tokens, width = dy_tokens.shape
    rows = pre_act.shape[0]
    hidden_units = down_weight.shape[1]
    capacity = rows // experts
    assert capacity == FIRST + 1
    block_rows = capacity * width // LANES
    chips = replicas // 2
    assert chips & (chips - 1) == 0 and hidden_units % replicas == 0
    groups = 4
    period = chips // groups
    shape = jax.ShapeDtypeStruct
    vmem = pl.BlockSpec(memory_space=pltpu.VMEM)
    smem = pl.BlockSpec(memory_space=pltpu.SMEM)
    tail = pltpu.VMEM((experts, width // LANES, LANES), F32)
    block = shape((experts, block_rows, LANES), BF)

    outgoing, pick = pl.pallas_call(
        functools.partial(dispatch_kernel, experts),
        out_shape=(pltpu.HBM(block.shape, BF), shape((rows, tokens), BF)),
        in_specs=[pl.BlockSpec(memory_space=pl.ANY)] * 3,
        out_specs=(pl.BlockSpec(memory_space=pltpu.HBM), vmem),
        scratch_shapes=[
            pltpu.VMEM((tokens, width), BF),
            pltpu.VMEM(routing.T.shape, jnp.int32),
            pltpu.VMEM(route_weight.T.shape, F32),
            pltpu.VMEM((experts, block_rows, LANES), BF),
            tail,
            pltpu.SemaphoreType.DMA((7,)),
        ],
        compiler_params=PARAMS,
        name="dispatch_rows",
    )(*(pltpu.with_memory_space_constraint(x, pltpu.HBM) for x in (dy_tokens, routing.T, route_weight.T)))
    got = lax.all_to_all(outgoing, "expert", split_axis=0, concat_axis=0, tiled=True)

    own = lax.axis_index("dp")
    half = hidden_units // 2
    arrived, keep, send, factor = pl.pallas_call(
        functools.partial(partial_kernel, experts, chips, groups),
        out_shape=(
            shape((rows, width), BF),
            shape((half, width), F32),
            shape((half, width), BF),
            shape((rows, 2 * hidden_units), F32),
        ),
        in_specs=[smem, vmem, vmem],
        out_specs=(vmem,) * 4,
        scratch_shapes=[tail],
        compiler_params=PARAMS,
        name="down_partial",
    )(jnp.stack([own // 2, own % 2]), got, pre_act)
    other = lax.ppermute(send, "dp", [(i, i ^ 1) for i in range(replicas)])

    going_back = pl.pallas_call(
        functools.partial(grad_kernel, experts),
        out_shape=block,
        in_specs=[vmem] * 5,
        out_specs=vmem,
        scratch_shapes=[tail],
        compiler_params=PARAMS,
        name="grad_rows",
    )(arrived, factor, gate_weight, up_weight, down_weight)
    returned = lax.all_to_all(going_back, "expert", split_axis=0, concat_axis=0, tiled=True)

    total, coming, count, distance = keep, other, half, 1
    while distance < period:
        count //= 2
        going = (total[count:] + coming[count:].astype(F32)).astype(BF)
        hops = [
            (2 * z + c, 2 * ((z + (distance if c == 0 else -distance)) % chips) + c)
            for z in range(chips)
            for c in range(2)
        ]
        total = lax.optimization_barrier(total[:count] + coming[:count].astype(F32))
        coming = lax.ppermute(going, "dp", hops)
        distance *= 2
    share = hidden_units // replicas
    lines = share * width // LANES
    going = pl.pallas_call(
        fold_kernel,
        out_shape=shape((groups, lines, LANES), BF),
        in_specs=[vmem] * 2,
        out_specs=vmem,
        scratch_shapes=[pltpu.VMEM((count, width // LANES, LANES), F32)],
        compiler_params=PARAMS,
        name="fold",
    )(total, coming)
    members = [[2 * (g * period + i) + c for g in range(groups)] for i in range(period) for c in range(2)]
    coming = lax.all_to_all(going, "dp", 0, 0, axis_index_groups=members, tiled=True)
    grad_tokens = pl.pallas_call(
        functools.partial(combine_kernel, experts),
        out_shape=shape((tokens, width), BF),
        in_specs=[vmem] * 2,
        out_specs=vmem,
        scratch_shapes=[tail],
        compiler_params=PARAMS,
        name="combine_rows",
    )(pick, returned)
    coming, grad_tokens = lax.optimization_barrier((coming, grad_tokens))
    grad_down = pl.pallas_call(
        functools.partial(finish_kernel, 1.0 / replicas),
        out_shape=shape((1, share, width), F32),
        in_specs=[vmem],
        out_specs=vmem,
        scratch_shapes=[pltpu.VMEM((share, width // LANES, LANES), F32)],
        compiler_params=PARAMS,
        name="finish",
    )(coming)
    return (grad_tokens, grad_down)


def solution(mesh):
    placed = (
        P(("dp", "expert"), None),
        P(("dp", "expert"), None),
        P(("dp", "expert"), None),
        P(("dp", "expert"), None),
        P("expert", None, None),
        P("expert", None, None),
        P("expert", None, None),
    )
    return jax.shard_map(
        per_device,
        mesh=mesh,
        in_specs=placed,
        out_specs=(P(("dp", "expert"), None), P("expert", "dp", None)),
        check_vma=False,
    )
```

```python
import functools

import jax
import jax.numpy as jnp
from jax import lax
from jax.experimental import pallas as pl
from jax.experimental.pallas import tpu as pltpu
from jax.sharding import PartitionSpec as P

BF = jnp.bfloat16
F32 = jnp.float32
LANES = 128
FIRST = 8
PARTS = 4
PARAMS = pltpu.CompilerParams(vmem_limit_bytes=16 * 1024 * 1024)


def dot(a, b, contract):
    return lax.dot_general(a, b, (contract, ((), ())), preferred_element_type=F32)


def iota(shape, axis):
    return lax.broadcasted_iota(jnp.int32, shape, axis)


def write_block(ref, tail, pair, first, second, experts):
    main = experts * FIRST
    tiles = [x[:main].reshape(experts, FIRST, LANES) for x in (first, second)]
    ref[:, pair * 16 : pair * 16 + 16, :] = jnp.concatenate(tiles, axis=1).astype(BF)
    tail[:, 2 * pair, :] = first[main:]
    tail[:, 2 * pair + 1, :] = second[main:]


def read_block(ref, tail, pair, experts):
    both = ref[:, pair * 16 : pair * 16 + 16, :].astype(F32)
    main = experts * FIRST
    halves = []
    for at in range(2):
        block = both[:, at * FIRST : (at + 1) * FIRST, :].reshape(main, LANES)
        halves.append(jnp.concatenate([block, tail[:, 2 * pair + at, :]], axis=0))
    return jnp.concatenate(halves, axis=1)


def dispatch_kernel(
    experts, dy_hbm, routing_hbm, weight_hbm, out_hbm, pick_ref, dy_ref, routing_ref, weight_ref, out_ref, tail, sems
):
    loads = [
        pltpu.make_async_copy(source, target, sems.at[i])
        for i, (source, target) in enumerate(
            [(routing_hbm, routing_ref), (weight_hbm, weight_ref), (dy_hbm, dy_ref)]
        )
    ]
    for load in loads:
        load.start()
    loads[0].wait()
    loads[1].wait()
    tokens, width = dy_ref.shape
    route_count = routing_ref.shape[0]
    main = experts * FIRST
    rows = main + experts
    slot = iota((rows, tokens), 0)
    expert = jnp.where(slot < main, slot // FIRST, slot - main)
    position = jnp.where(slot < main, slot % FIRST, FIRST)
    named = jnp.zeros((rows, tokens), F32)
    scale = jnp.zeros((rows, tokens), F32)
    for k in range(route_count):
        hit = routing_ref[k : k + 1, :] == expert
        named = named + jnp.where(hit, 1.0, 0.0)
        scale = scale + jnp.where(hit, weight_ref[k : k + 1, :], 0.0)
    earlier = jnp.where(iota((tokens, tokens), 0) < iota((tokens, tokens), 1), 1.0, 0.0)
    before = dot(named.astype(BF), earlier.astype(BF), ((1,), (0,)))
    pick = jnp.where((named > 0.5) & (before == position.astype(F32)), 1.0, 0.0)
    chosen = pick.astype(BF)
    pick_ref[...] = chosen
    row_weight = jnp.sum(pick * scale, axis=1, keepdims=True)
    loads[2].wait()

    def columns(at):
        return dot(chosen, dy_ref[:, at], ((1,), (0,))) * row_weight

    write_all(columns, width, experts, out_ref, out_hbm, tail, [sems.at[3 + i] for i in range(PARTS)])


def write_all(columns, width, experts, out_ref, out_hbm, tail, sems):
    pairs = width // (2 * LANES)
    step = pairs // PARTS
    stores = []
    for pair in range(pairs):
        part = columns(slice(pair * 2 * LANES, (pair + 1) * 2 * LANES))
        write_block(out_ref, tail, pair, part[:, :LANES], part[:, LANES:], experts)
        if (pair + 1) % step == 0:
            stop = (pair + 1) * 16
            if pair + 1 == pairs:
                out_ref[:, stop:, :] = tail[...].astype(BF)
                stop = out_ref.shape[1]
            rows = slice(len(stores) * step * 16, stop)
            stores.append(
                pltpu.make_async_copy(
                    out_ref.at[:, rows, :], out_hbm.at[:, rows, :], sems[len(stores)]
                )
            )
            stores[-1].start()
    for store in stores:
        store.wait()


def experts_rows(width):
    return width // LANES * FIRST


def partial_kernel(
    experts, chips, at_ref, got_ref, pre_ref, arrived_ref, keep_ref, send_ref, factor_ref, tail
):
    rows, width = arrived_ref.shape
    hidden_units = pre_ref.shape[1] // 2
    main = experts * FIRST
    capacity = rows // experts
    new, old = iota((rows, rows), 0), iota((rows, rows), 1)
    source = jnp.where(
        new < main, new // FIRST * capacity + new % FIRST, (new - main) * capacity + FIRST
    )
    order = jnp.where(source == old, 1.0, 0.0).astype(BF)
    pre = dot(order, pre_ref[...], ((1,), (0,)))
    gate_pre, up_pre = pre[:, :hidden_units], pre[:, hidden_units:]
    sigmoid = 1.0 / (1.0 + jnp.exp(-gate_pre))
    activated = gate_pre * sigmoid
    factor_ref[:, :hidden_units] = up_pre * sigmoid * (1.0 + gate_pre * (1.0 - sigmoid))
    factor_ref[:, hidden_units:] = activated
    hidden = (activated * up_pre).astype(BF)
    half = hidden_units // 2
    unit, at = iota((hidden_units, hidden_units), 0), iota((hidden_units, hidden_units), 1)
    core = jnp.where(at < half, at_ref[1], 1 - at_ref[1])
    share = half // chips
    place = at % half // share
    far = jnp.zeros_like(place)
    bits = chips.bit_length() - 1
    for bit in range(bits):
        far = far + (place // 2**bit) % 2 * 2 ** (bits - 1 - bit)
    chip = (at_ref[0] + (1 - 2 * core) * far + chips) % chips
    target = (2 * chip + core) * share + at % share
    hidden = dot(hidden, jnp.where(unit == target, 1.0, 0.0).astype(BF), ((1,), (0,))).astype(BF)
    tail[...] = got_ref[:, experts_rows(width) :, :].astype(F32)
    for pair in range(width // (2 * LANES)):
        at = slice(pair * 2 * LANES, (pair + 1) * 2 * LANES)
        arrived = read_block(got_ref, tail, pair, experts).astype(BF)
        arrived_ref[:, at] = arrived
        part = dot(hidden, arrived, ((0,), (0,)))
        keep_ref[:, at] = part[:half]
        send_ref[:, at] = part[half:].astype(BF)


def hidden_kernel(arrived_ref, factor_ref, down_ref, out_ref):
    grad_hidden = dot(arrived_ref[...], down_ref[0], ((1,), (1,)))
    out_ref[...] = (jnp.concatenate([grad_hidden, grad_hidden], axis=1) * factor_ref[...]).astype(BF)


def grad_kernel(experts, hidden_ref, gate_ref, up_ref, out_hbm, out_ref, tail, sems):
    hidden = hidden_ref[...]

    def columns(at):
        weight = jnp.concatenate([gate_ref[0, at, :], up_ref[0, at, :]], axis=1)
        return dot(hidden, weight, ((1,), (1,)))

    write_all(columns, gate_ref.shape[1], experts, out_ref, out_hbm, tail, [sems.at[i] for i in range(PARTS)])


def combine_kernel(experts, pick_ref, got_ref, out_ref, tail):
    width = out_ref.shape[1]
    tail[...] = got_ref[:, experts_rows(width) :, :].astype(F32)
    pick = pick_ref[...]
    for pair in range(width // (2 * LANES)):
        rows = read_block(got_ref, tail, pair, experts).astype(BF)
        out_ref[:, pair * 2 * LANES : (pair + 1) * 2 * LANES] = dot(
            pick, rows, ((0,), (0,))
        ).astype(BF)


def fold_kernel(total_ref, coming_ref, keep_ref, send_ref, lines):
    for c in range(lines.shape[1]):
        at = slice(c * LANES, (c + 1) * LANES)
        lines[:, c, :] = total_ref[:, at] + coming_ref[:, at].astype(F32)
    count = keep_ref.shape[0]
    pieces = lines[...].reshape((2 * count,) + keep_ref.shape[1:])
    keep_ref[...] = pieces[:count]
    send_ref[...] = pieces[count:].astype(BF)


def finish_kernel(scale, total_ref, coming_ref, out_ref, lines):
    lines[...] = ((total_ref[0] + coming_ref[0].astype(F32)) * scale).reshape(lines.shape)
    for c in range(lines.shape[1]):
        out_ref[0, :, c * LANES : (c + 1) * LANES] = lines[:, c, :]


def per_device(dy_tokens, routing, route_weight, pre_act, gate_weight, up_weight, down_weight):
    experts = lax.axis_size("expert")
    replicas = lax.axis_size("dp")
    tokens, width = dy_tokens.shape
    rows = pre_act.shape[0]
    hidden_units = down_weight.shape[1]
    capacity = rows // experts
    assert capacity == FIRST + 1
    block_rows = capacity * width // LANES
    chips = replicas // 2
    assert chips & (chips - 1) == 0 and hidden_units % replicas == 0
    shape = jax.ShapeDtypeStruct
    vmem = pl.BlockSpec(memory_space=pltpu.VMEM)
    smem = pl.BlockSpec(memory_space=pltpu.SMEM)
    tail = pltpu.VMEM((experts, width // LANES, LANES), F32)
    block = shape((experts, block_rows, LANES), BF)

    outgoing, pick = pl.pallas_call(
        functools.partial(dispatch_kernel, experts),
        out_shape=(pltpu.HBM(block.shape, BF), shape((rows, tokens), BF)),
        in_specs=[pl.BlockSpec(memory_space=pl.ANY)] * 3,
        out_specs=(pl.BlockSpec(memory_space=pltpu.HBM), vmem),
        scratch_shapes=[
            pltpu.VMEM((tokens, width), BF),
            pltpu.VMEM(routing.T.shape, jnp.int32),
            pltpu.VMEM(route_weight.T.shape, F32),
            pltpu.VMEM((experts, block_rows, LANES), BF),
            tail,
            pltpu.SemaphoreType.DMA((3 + PARTS,)),
        ],
        compiler_params=PARAMS,
        name="dispatch_rows",
    )(*(pltpu.with_memory_space_constraint(x, pltpu.HBM) for x in (dy_tokens, routing.T, route_weight.T)))
    got = lax.all_to_all(outgoing, "expert", split_axis=0, concat_axis=0, tiled=True)

    own = lax.axis_index("dp")
    half = hidden_units // 2
    arrived, keep, send, factor = pl.pallas_call(
        functools.partial(partial_kernel, experts, chips),
        out_shape=(
            shape((rows, width), BF),
            shape((half, width), F32),
            shape((half, width), BF),
            shape((rows, 2 * hidden_units), F32),
        ),
        in_specs=[smem, vmem, vmem],
        out_specs=(vmem,) * 4,
        scratch_shapes=[tail],
        compiler_params=PARAMS,
        name="down_partial",
    )(jnp.stack([own // 2, own % 2]), got, pre_act)
    other = lax.ppermute(send, "dp", [(i, i ^ 1) for i in range(replicas)])

    grad_hidden = pl.pallas_call(
        hidden_kernel,
        out_shape=shape((rows, 2 * hidden_units), BF),
        in_specs=[vmem] * 3,
        out_specs=vmem,
        compiler_params=PARAMS,
        name="grad_hidden",
    )(arrived, factor, down_weight)
    other, grad_hidden = lax.optimization_barrier((other, grad_hidden))
    going_back = pl.pallas_call(
        functools.partial(grad_kernel, experts),
        out_shape=pltpu.HBM(block.shape, BF),
        in_specs=[vmem] * 3,
        out_specs=pl.BlockSpec(memory_space=pltpu.HBM),
        scratch_shapes=[
            pltpu.VMEM((experts, block_rows, LANES), BF),
            tail,
            pltpu.SemaphoreType.DMA((PARTS,)),
        ],
        compiler_params=PARAMS,
        name="grad_rows",
    )(grad_hidden, gate_weight, up_weight)
    def pass_on(going, distance):
        hops = [
            (2 * z + c, 2 * ((z + (distance if c == 0 else -distance)) % chips) + c)
            for z in range(chips)
            for c in range(2)
        ]
        return lax.ppermute(going, "dp", hops)

    share = hidden_units // replicas
    lines = share * width // LANES
    total, coming, count, distance = keep, other, half, 1
    while count > 8:
        count //= 2
        going = (total[count:] + coming[count:].astype(F32)).astype(BF)
        total = lax.optimization_barrier(total[:count] + coming[:count].astype(F32))
        coming = pass_on(going, distance)
        if distance == 1:
            coming, going_back = lax.optimization_barrier((coming, going_back))
        distance *= 2
    returned = lax.all_to_all(going_back, "expert", split_axis=0, concat_axis=0, tiled=True)
    count = count // share // 2
    total, going = pl.pallas_call(
        fold_kernel,
        out_shape=(shape((count, lines, LANES), F32), shape((count, lines, LANES), BF)),
        in_specs=[vmem] * 2,
        out_specs=(vmem, vmem),
        scratch_shapes=[pltpu.VMEM((2 * count * share, width // LANES, LANES), F32)],
        compiler_params=PARAMS,
        name="fold",
    )(total, coming)
    coming = pass_on(going, distance)
    while count > 1:
        count //= 2
        distance *= 2
        going = (total[count:] + coming[count:].astype(F32)).astype(BF)
        total = lax.optimization_barrier(total[:count] + coming[:count].astype(F32))
        coming = pass_on(going, distance)
    grad_tokens = pl.pallas_call(
        functools.partial(combine_kernel, experts),
        out_shape=shape((tokens, width), BF),
        in_specs=[vmem] * 2,
        out_specs=vmem,
        scratch_shapes=[tail],
        compiler_params=PARAMS,
        name="combine_rows",
    )(pick, returned)
    coming, grad_tokens = lax.optimization_barrier((coming, grad_tokens))
    grad_down = pl.pallas_call(
        functools.partial(finish_kernel, 1.0 / replicas),
        out_shape=shape((1, share, width), F32),
        in_specs=[vmem] * 2,
        out_specs=vmem,
        scratch_shapes=[pltpu.VMEM((share, width // LANES, LANES), F32)],
        compiler_params=PARAMS,
        name="finish",
    )(total, coming)
    return (grad_tokens, grad_down)


def solution(mesh):
    placed = (
        P(("dp", "expert"), None),
        P(("dp", "expert"), None),
        P(("dp", "expert"), None),
        P(("dp", "expert"), None),
        P("expert", None, None),
        P("expert", None, None),
        P("expert", None, None),
    )
    return jax.shard_map(
        per_device,
        mesh=mesh,
        in_specs=placed,
        out_specs=(P(("dp", "expert"), None), P("expert", "dp", None)),
        check_vma=False,
    )
```

```python
import functools

import jax
import jax.numpy as jnp
from jax import lax
from jax.experimental import pallas as pl
from jax.experimental.pallas import tpu as pltpu
from jax.sharding import PartitionSpec as P

BF = jnp.bfloat16
F32 = jnp.float32
LANES = 128
FIRST = 8
PARTS = 4
HOPS = (1, -2, 4)
RING = 4
PARAMS = pltpu.CompilerParams(vmem_limit_bytes=16 * 1024 * 1024)


def dot(a, b, contract):
    return lax.dot_general(a, b, (contract, ((), ())), preferred_element_type=F32)


def iota(shape, axis):
    return lax.broadcasted_iota(jnp.int32, shape, axis)


def write_block(ref, tail, pair, first, second, experts):
    main = experts * FIRST
    tiles = [x[:main].reshape(experts, FIRST, LANES) for x in (first, second)]
    ref[:, pair * 16 : pair * 16 + 16, :] = jnp.concatenate(tiles, axis=1).astype(BF)
    tail[:, 2 * pair, :] = first[main:]
    tail[:, 2 * pair + 1, :] = second[main:]


def read_block(ref, tail, pair, experts):
    both = ref[:, pair * 16 : pair * 16 + 16, :].astype(F32)
    main = experts * FIRST
    halves = []
    for at in range(2):
        block = both[:, at * FIRST : (at + 1) * FIRST, :].reshape(main, LANES)
        halves.append(jnp.concatenate([block, tail[:, 2 * pair + at, :]], axis=0))
    return jnp.concatenate(halves, axis=1)


def dispatch_kernel(
    experts, dy_hbm, routing_hbm, weight_hbm, out_hbm, pick_ref, dy_ref, routing_ref, weight_ref, out_ref, tail, sems
):
    loads = [
        pltpu.make_async_copy(source, target, sems.at[i])
        for i, (source, target) in enumerate(
            [(routing_hbm, routing_ref), (weight_hbm, weight_ref), (dy_hbm, dy_ref)]
        )
    ]
    for load in loads:
        load.start()
    loads[0].wait()
    loads[1].wait()
    tokens, width = dy_ref.shape
    route_count = routing_ref.shape[0]
    main = experts * FIRST
    rows = main + experts
    slot = iota((rows, tokens), 0)
    expert = jnp.where(slot < main, slot // FIRST, slot - main)
    position = jnp.where(slot < main, slot % FIRST, FIRST)
    named = jnp.zeros((rows, tokens), F32)
    scale = jnp.zeros((rows, tokens), F32)
    for k in range(route_count):
        hit = routing_ref[k : k + 1, :] == expert
        named = named + jnp.where(hit, 1.0, 0.0)
        scale = scale + jnp.where(hit, weight_ref[k : k + 1, :], 0.0)
    earlier = jnp.where(iota((tokens, tokens), 0) < iota((tokens, tokens), 1), 1.0, 0.0)
    before = dot(named.astype(BF), earlier.astype(BF), ((1,), (0,)))
    pick = jnp.where((named > 0.5) & (before == position.astype(F32)), 1.0, 0.0)
    chosen = pick.astype(BF)
    pick_ref[...] = chosen
    row_weight = jnp.sum(pick * scale, axis=1, keepdims=True)
    loads[2].wait()

    def columns(at):
        return dot(chosen, dy_ref[:, at], ((1,), (0,))) * row_weight

    write_all(columns, width, experts, out_ref, out_hbm, tail, [sems.at[3 + i] for i in range(PARTS)])


def write_all(columns, width, experts, out_ref, out_hbm, tail, sems):
    pairs = width // (2 * LANES)
    step = pairs // PARTS
    stores = []
    for pair in range(pairs):
        part = columns(slice(pair * 2 * LANES, (pair + 1) * 2 * LANES))
        write_block(out_ref, tail, pair, part[:, :LANES], part[:, LANES:], experts)
        if (pair + 1) % step == 0:
            stop = (pair + 1) * 16
            if pair + 1 == pairs:
                out_ref[:, stop:, :] = tail[...].astype(BF)
                stop = out_ref.shape[1]
            rows = slice(len(stores) * step * 16, stop)
            stores.append(
                pltpu.make_async_copy(
                    out_ref.at[:, rows, :], out_hbm.at[:, rows, :], sems[len(stores)]
                )
            )
            stores[-1].start()
    for store in stores:
        store.wait()


def experts_rows(width):
    return width // LANES * FIRST


def partial_kernel(
    experts, chips, at_ref, got_ref, pre_ref, arrived_ref, keep_ref, send_ref, factor_ref, tail
):
    rows, width = arrived_ref.shape
    hidden_units = pre_ref.shape[1] // 2
    main = experts * FIRST
    capacity = rows // experts
    new, old = iota((rows, rows), 0), iota((rows, rows), 1)
    source = jnp.where(
        new < main, new // FIRST * capacity + new % FIRST, (new - main) * capacity + FIRST
    )
    order = jnp.where(source == old, 1.0, 0.0).astype(BF)
    pre = dot(order, pre_ref[...], ((1,), (0,)))
    gate_pre, up_pre = pre[:, :hidden_units], pre[:, hidden_units:]
    sigmoid = 1.0 / (1.0 + jnp.exp(-gate_pre))
    activated = gate_pre * sigmoid
    factor_ref[:, :hidden_units] = up_pre * sigmoid * (1.0 + gate_pre * (1.0 - sigmoid))
    factor_ref[:, hidden_units:] = activated
    hidden = (activated * up_pre).astype(BF)
    half = hidden_units // 2
    unit, at = iota((hidden_units, hidden_units), 0), iota((hidden_units, hidden_units), 1)
    core = jnp.where(at < half, at_ref[1], 1 - at_ref[1])
    share = half // chips
    place = at % half // share
    far = place % RING * (HOPS[-1] * 2 * -1)
    for bit, hop in enumerate(reversed(HOPS)):
        far = far + place // (RING * 2**bit) % 2 * hop
    chip = (at_ref[0] + (1 - 2 * core) * far + 2 * chips) % chips
    target = (2 * chip + core) * share + at % share
    hidden = dot(hidden, jnp.where(unit == target, 1.0, 0.0).astype(BF), ((1,), (0,))).astype(BF)
    tail[...] = got_ref[:, experts_rows(width) :, :].astype(F32)
    for pair in range(width // (2 * LANES)):
        at = slice(pair * 2 * LANES, (pair + 1) * 2 * LANES)
        arrived = read_block(got_ref, tail, pair, experts).astype(BF)
        arrived_ref[:, at] = arrived
        part = dot(hidden, arrived, ((0,), (0,)))
        keep_ref[:, at] = part[:half]
        send_ref[:, at] = part[half:].astype(BF)


def hidden_kernel(arrived_ref, factor_ref, down_ref, out_ref):
    grad_hidden = dot(arrived_ref[...], down_ref[0], ((1,), (1,)))
    out_ref[...] = (jnp.concatenate([grad_hidden, grad_hidden], axis=1) * factor_ref[...]).astype(BF)


def grad_kernel(experts, hidden_ref, gate_ref, up_ref, out_hbm, out_ref, tail, sems):
    hidden = hidden_ref[...]

    def columns(at):
        weight = jnp.concatenate([gate_ref[0, at, :], up_ref[0, at, :]], axis=1)
        return dot(hidden, weight, ((1,), (1,)))

    write_all(columns, gate_ref.shape[1], experts, out_ref, out_hbm, tail, [sems.at[i] for i in range(PARTS)])


def combine_kernel(experts, pick_ref, got_ref, out_ref, tail):
    width = out_ref.shape[1]
    tail[...] = got_ref[:, experts_rows(width) :, :].astype(F32)
    pick = pick_ref[...]
    for pair in range(width // (2 * LANES)):
        rows = read_block(got_ref, tail, pair, experts).astype(BF)
        out_ref[:, pair * 2 * LANES : (pair + 1) * 2 * LANES] = dot(
            pick, rows, ((0,), (0,))
        ).astype(BF)


def fold_kernel(total_ref, coming_ref, own_ref, next_ref, opposite_ref, previous_ref, lines):
    for c in range(lines.shape[1]):
        at = slice(c * LANES, (c + 1) * LANES)
        lines[:, c, :] = total_ref[:, at] + coming_ref[:, at].astype(F32)
    pieces = lines[...].reshape((RING,) + own_ref.shape)
    own_ref[...] = pieces[0]
    next_ref[...] = pieces[1].astype(BF)
    opposite_ref[...] = pieces[2].astype(BF)
    previous_ref[...] = pieces[3].astype(BF)


def finish_kernel(scale, own_ref, *refs):
    *coming, out_ref, lines = refs
    total = own_ref[...]
    for ref in coming:
        total = total + ref[...].astype(F32)
    lines[...] = (total * scale).reshape(lines.shape)
    for c in range(lines.shape[1]):
        out_ref[0, :, c * LANES : (c + 1) * LANES] = lines[:, c, :]


def per_device(dy_tokens, routing, route_weight, pre_act, gate_weight, up_weight, down_weight):
    experts = lax.axis_size("expert")
    replicas = lax.axis_size("dp")
    tokens, width = dy_tokens.shape
    rows = pre_act.shape[0]
    hidden_units = down_weight.shape[1]
    capacity = rows // experts
    assert capacity == FIRST + 1
    block_rows = capacity * width // LANES
    chips = replicas // 2
    assert chips == 2 ** len(HOPS) * RING and hidden_units % replicas == 0
    shape = jax.ShapeDtypeStruct
    vmem = pl.BlockSpec(memory_space=pltpu.VMEM)
    smem = pl.BlockSpec(memory_space=pltpu.SMEM)
    tail = pltpu.VMEM((experts, width // LANES, LANES), F32)
    block = shape((experts, block_rows, LANES), BF)

    outgoing, pick = pl.pallas_call(
        functools.partial(dispatch_kernel, experts),
        out_shape=(pltpu.HBM(block.shape, BF), shape((rows, tokens), BF)),
        in_specs=[pl.BlockSpec(memory_space=pl.ANY)] * 3,
        out_specs=(pl.BlockSpec(memory_space=pltpu.HBM), vmem),
        scratch_shapes=[
            pltpu.VMEM((tokens, width), BF),
            pltpu.VMEM(routing.T.shape, jnp.int32),
            pltpu.VMEM(route_weight.T.shape, F32),
            pltpu.VMEM((experts, block_rows, LANES), BF),
            tail,
            pltpu.SemaphoreType.DMA((3 + PARTS,)),
        ],
        compiler_params=PARAMS,
        name="dispatch_rows",
    )(*(pltpu.with_memory_space_constraint(x, pltpu.HBM) for x in (dy_tokens, routing.T, route_weight.T)))
    got = lax.all_to_all(outgoing, "expert", split_axis=0, concat_axis=0, tiled=True)

    own = lax.axis_index("dp")
    half = hidden_units // 2
    arrived, keep, send, factor = pl.pallas_call(
        functools.partial(partial_kernel, experts, chips),
        out_shape=(
            shape((rows, width), BF),
            shape((half, width), F32),
            shape((half, width), BF),
            shape((rows, 2 * hidden_units), F32),
        ),
        in_specs=[smem, vmem, vmem],
        out_specs=(vmem,) * 4,
        scratch_shapes=[tail],
        compiler_params=PARAMS,
        name="down_partial",
    )(jnp.stack([own // 2, own % 2]), got, pre_act)
    other = lax.ppermute(send, "dp", [(i, i ^ 1) for i in range(replicas)])

    grad_hidden = pl.pallas_call(
        hidden_kernel,
        out_shape=shape((rows, 2 * hidden_units), BF),
        in_specs=[vmem] * 3,
        out_specs=vmem,
        compiler_params=PARAMS,
        name="grad_hidden",
    )(arrived, factor, down_weight)
    other, grad_hidden = lax.optimization_barrier((other, grad_hidden))
    going_back = pl.pallas_call(
        functools.partial(grad_kernel, experts),
        out_shape=pltpu.HBM(block.shape, BF),
        in_specs=[vmem] * 3,
        out_specs=pl.BlockSpec(memory_space=pltpu.HBM),
        scratch_shapes=[
            pltpu.VMEM((experts, block_rows, LANES), BF),
            tail,
            pltpu.SemaphoreType.DMA((PARTS,)),
        ],
        compiler_params=PARAMS,
        name="grad_rows",
    )(grad_hidden, gate_weight, up_weight)
    def pass_on(going, distance):
        hops = [
            (2 * z + c, 2 * ((z + (distance if c == 0 else -distance)) % chips) + c)
            for z in range(chips)
            for c in range(2)
        ]
        return lax.ppermute(going, "dp", hops)

    share = hidden_units // replicas
    total, coming, count = keep, other, half
    for hop in HOPS:
        count //= 2
        going = (total[count:] + coming[count:].astype(F32)).astype(BF)
        total = lax.optimization_barrier(total[:count] + coming[:count].astype(F32))
        coming = pass_on(going, hop)
        if hop == HOPS[0]:
            coming, going_back = lax.optimization_barrier((coming, going_back))
    returned = lax.all_to_all(going_back, "expert", split_axis=0, concat_axis=0, tiled=True)
    piece = (share * width // LANES, LANES)
    own, ahead, opposite, previous = pl.pallas_call(
        fold_kernel,
        out_shape=(shape(piece, F32),) + (shape(piece, BF),) * 3,
        in_specs=[vmem] * 2,
        out_specs=(vmem,) * 4,
        scratch_shapes=[pltpu.VMEM((count, width // LANES, LANES), F32)],
        compiler_params=PARAMS,
        name="fold",
    )(total, coming)
    stride = -2 * HOPS[-1]
    parts = [pass_on(opposite, 2 * stride), pass_on(ahead, stride), pass_on(previous, -stride)]
    grad_tokens = pl.pallas_call(
        functools.partial(combine_kernel, experts),
        out_shape=shape((tokens, width), BF),
        in_specs=[vmem] * 2,
        out_specs=vmem,
        scratch_shapes=[tail],
        compiler_params=PARAMS,
        name="combine_rows",
    )(pick, returned)
    parts[0], grad_tokens = lax.optimization_barrier((parts[0], grad_tokens))
    grad_down = pl.pallas_call(
        functools.partial(finish_kernel, 1.0 / replicas),
        out_shape=shape((1, share, width), F32),
        in_specs=[vmem] * RING,
        out_specs=vmem,
        scratch_shapes=[pltpu.VMEM((share, width // LANES, LANES), F32)],
        compiler_params=PARAMS,
        name="finish",
    )(own, *parts)
    return (grad_tokens, grad_down)


def solution(mesh):
    placed = (
        P(("dp", "expert"), None),
        P(("dp", "expert"), None),
        P(("dp", "expert"), None),
        P(("dp", "expert"), None),
        P("expert", None, None),
        P("expert", None, None),
        P("expert", None, None),
    )
    return jax.shard_map(
        per_device,
        mesh=mesh,
        in_specs=placed,
        out_specs=(P(("dp", "expert"), None), P("expert", "dp", None)),
        check_vma=False,
    )
```

```python
import functools

import jax
import jax.numpy as jnp
from jax import lax
from jax.experimental import pallas as pl
from jax.experimental.pallas import tpu as pltpu
from jax.sharding import PartitionSpec as P

BF = jnp.bfloat16
F32 = jnp.float32
LANES = 128
FIRST = 8
PARTS = 4
NEAR = (0, -2, -4, 2)
FAR = (0, 8, 16, -8)
PARAMS = pltpu.CompilerParams(vmem_limit_bytes=16 * 1024 * 1024)


def dot(a, b, contract):
    return lax.dot_general(a, b, (contract, ((), ())), preferred_element_type=F32)


def iota(shape, axis):
    return lax.broadcasted_iota(jnp.int32, shape, axis)


def write_block(ref, tail, pair, first, second, experts):
    main = experts * FIRST
    tiles = [x[:main].reshape(experts, FIRST, LANES) for x in (first, second)]
    ref[:, pair * 16 : pair * 16 + 16, :] = jnp.concatenate(tiles, axis=1).astype(BF)
    tail[:, 2 * pair, :] = first[main:]
    tail[:, 2 * pair + 1, :] = second[main:]


def read_block(ref, tail, pair, experts):
    both = ref[:, pair * 16 : pair * 16 + 16, :].astype(F32)
    main = experts * FIRST
    halves = []
    for at in range(2):
        block = both[:, at * FIRST : (at + 1) * FIRST, :].reshape(main, LANES)
        halves.append(jnp.concatenate([block, tail[:, 2 * pair + at, :]], axis=0))
    return jnp.concatenate(halves, axis=1)


def dispatch_kernel(
    experts, dy_hbm, routing_hbm, weight_hbm, out_hbm, pick_ref, dy_ref, routing_ref, weight_ref, out_ref, tail, sems
):
    loads = [
        pltpu.make_async_copy(source, target, sems.at[i])
        for i, (source, target) in enumerate(
            [(routing_hbm, routing_ref), (weight_hbm, weight_ref), (dy_hbm, dy_ref)]
        )
    ]
    for load in loads:
        load.start()
    loads[0].wait()
    loads[1].wait()
    tokens, width = dy_ref.shape
    route_count = routing_ref.shape[0]
    main = experts * FIRST
    rows = main + experts
    slot = iota((rows, tokens), 0)
    expert = jnp.where(slot < main, slot // FIRST, slot - main)
    position = jnp.where(slot < main, slot % FIRST, FIRST)
    named = jnp.zeros((rows, tokens), F32)
    scale = jnp.zeros((rows, tokens), F32)
    for k in range(route_count):
        hit = routing_ref[k : k + 1, :] == expert
        named = named + jnp.where(hit, 1.0, 0.0)
        scale = scale + jnp.where(hit, weight_ref[k : k + 1, :], 0.0)
    earlier = jnp.where(iota((tokens, tokens), 0) < iota((tokens, tokens), 1), 1.0, 0.0)
    before = dot(named.astype(BF), earlier.astype(BF), ((1,), (0,)))
    pick = jnp.where((named > 0.5) & (before == position.astype(F32)), 1.0, 0.0)
    chosen = pick.astype(BF)
    pick_ref[...] = chosen
    row_weight = jnp.sum(pick * scale, axis=1, keepdims=True)
    loads[2].wait()

    def columns(at):
        return dot(chosen, dy_ref[:, at], ((1,), (0,))) * row_weight

    write_all(columns, width, experts, out_ref, out_hbm, tail, [sems.at[3 + i] for i in range(PARTS)])


def write_all(columns, width, experts, out_ref, out_hbm, tail, sems):
    pairs = width // (2 * LANES)
    step = pairs // PARTS
    stores = []
    for pair in range(pairs):
        part = columns(slice(pair * 2 * LANES, (pair + 1) * 2 * LANES))
        write_block(out_ref, tail, pair, part[:, :LANES], part[:, LANES:], experts)
        if (pair + 1) % step == 0:
            stop = (pair + 1) * 16
            if pair + 1 == pairs:
                out_ref[:, stop:, :] = tail[...].astype(BF)
                stop = out_ref.shape[1]
            rows = slice(len(stores) * step * 16, stop)
            stores.append(
                pltpu.make_async_copy(
                    out_ref.at[:, rows, :], out_hbm.at[:, rows, :], sems[len(stores)]
                )
            )
            stores[-1].start()
    for store in stores:
        store.wait()


def experts_rows(width):
    return width // LANES * FIRST


def partial_kernel(
    experts, chips, at_ref, got_ref, pre_ref, arrived_ref, keep_ref, send_ref, factor_ref, tail
):
    rows, width = arrived_ref.shape
    hidden_units = pre_ref.shape[1] // 2
    main = experts * FIRST
    capacity = rows // experts
    new, old = iota((rows, rows), 0), iota((rows, rows), 1)
    source = jnp.where(
        new < main, new // FIRST * capacity + new % FIRST, (new - main) * capacity + FIRST
    )
    order = jnp.where(source == old, 1.0, 0.0).astype(BF)
    pre = dot(order, pre_ref[...], ((1,), (0,)))
    gate_pre, up_pre = pre[:, :hidden_units], pre[:, hidden_units:]
    sigmoid = 1.0 / (1.0 + jnp.exp(-gate_pre))
    activated = gate_pre * sigmoid
    factor_ref[:, :hidden_units] = up_pre * sigmoid * (1.0 + gate_pre * (1.0 - sigmoid))
    factor_ref[:, hidden_units:] = activated
    hidden = (activated * up_pre).astype(BF)
    half = hidden_units // 2
    unit, at = iota((hidden_units, hidden_units), 0), iota((hidden_units, hidden_units), 1)
    core = jnp.where(at < half, at_ref[1], 1 - at_ref[1])
    share = half // chips
    place = at % half // share
    far = place // (len(NEAR) * len(FAR))
    for move in range(len(NEAR)):
        far = far + jnp.where(place // len(FAR) % len(NEAR) == move, NEAR[move], 0)
        far = far + jnp.where(place % len(FAR) == move, FAR[move], 0)
    chip = (at_ref[0] + (1 - 2 * core) * far + 2 * chips) % chips
    target = (2 * chip + core) * share + at % share
    hidden = dot(hidden, jnp.where(unit == target, 1.0, 0.0).astype(BF), ((1,), (0,))).astype(BF)
    tail[...] = got_ref[:, experts_rows(width) :, :].astype(F32)
    for pair in range(width // (2 * LANES)):
        at = slice(pair * 2 * LANES, (pair + 1) * 2 * LANES)
        arrived = read_block(got_ref, tail, pair, experts).astype(BF)
        arrived_ref[:, at] = arrived
        part = dot(hidden, arrived, ((0,), (0,)))
        keep_ref[:, at] = part[:half]
        send_ref[:, at] = part[half:].astype(BF)


def hidden_kernel(arrived_ref, factor_ref, down_ref, out_ref):
    grad_hidden = dot(arrived_ref[...], down_ref[0], ((1,), (1,)))
    out_ref[...] = (jnp.concatenate([grad_hidden, grad_hidden], axis=1) * factor_ref[...]).astype(BF)


def grad_kernel(experts, hidden_ref, gate_ref, up_ref, out_hbm, out_ref, tail, sems):
    hidden = hidden_ref[...]

    def columns(at):
        weight = jnp.concatenate([gate_ref[0, at, :], up_ref[0, at, :]], axis=1)
        return dot(hidden, weight, ((1,), (1,)))

    write_all(columns, gate_ref.shape[1], experts, out_ref, out_hbm, tail, [sems.at[i] for i in range(PARTS)])


def combine_kernel(experts, pick_ref, got_ref, out_ref, tail):
    width = out_ref.shape[1]
    tail[...] = got_ref[:, experts_rows(width) :, :].astype(F32)
    pick = pick_ref[...]
    for pair in range(width // (2 * LANES)):
        rows = read_block(got_ref, tail, pair, experts).astype(BF)
        out_ref[:, pair * 2 * LANES : (pair + 1) * 2 * LANES] = dot(
            pick, rows, ((0,), (0,))
        ).astype(BF)


def fold_kernel(total_ref, *refs):
    *coming, own_ref, first_ref, second_ref, third_ref, lines = refs
    for c in range(lines.shape[1]):
        at = slice(c * LANES, (c + 1) * LANES)
        total = total_ref[:, at]
        for ref in coming:
            total = total + ref[:, at].astype(F32)
        lines[:, c, :] = total
    pieces = lines[...].reshape((len(FAR),) + own_ref.shape)
    own_ref[...] = pieces[0]
    first_ref[...] = pieces[1].astype(BF)
    second_ref[...] = pieces[2].astype(BF)
    third_ref[...] = pieces[3].astype(BF)


def finish_kernel(scale, own_ref, *refs):
    *coming, out_ref, lines = refs
    total = own_ref[...]
    for ref in coming:
        total = total + ref[...].astype(F32)
    lines[...] = (total * scale).reshape(lines.shape)
    for c in range(lines.shape[1]):
        out_ref[0, :, c * LANES : (c + 1) * LANES] = lines[:, c, :]


def per_device(dy_tokens, routing, route_weight, pre_act, gate_weight, up_weight, down_weight):
    experts = lax.axis_size("expert")
    replicas = lax.axis_size("dp")
    tokens, width = dy_tokens.shape
    rows = pre_act.shape[0]
    hidden_units = down_weight.shape[1]
    capacity = rows // experts
    assert capacity == FIRST + 1
    block_rows = capacity * width // LANES
    chips = replicas // 2
    assert chips == 2 * len(NEAR) * len(FAR) and hidden_units % replicas == 0
    shape = jax.ShapeDtypeStruct
    vmem = pl.BlockSpec(memory_space=pltpu.VMEM)
    smem = pl.BlockSpec(memory_space=pltpu.SMEM)
    tail = pltpu.VMEM((experts, width // LANES, LANES), F32)
    block = shape((experts, block_rows, LANES), BF)

    outgoing, pick = pl.pallas_call(
        functools.partial(dispatch_kernel, experts),
        out_shape=(pltpu.HBM(block.shape, BF), shape((rows, tokens), BF)),
        in_specs=[pl.BlockSpec(memory_space=pl.ANY)] * 3,
        out_specs=(pl.BlockSpec(memory_space=pltpu.HBM), vmem),
        scratch_shapes=[
            pltpu.VMEM((tokens, width), BF),
            pltpu.VMEM(routing.T.shape, jnp.int32),
            pltpu.VMEM(route_weight.T.shape, F32),
            pltpu.VMEM((experts, block_rows, LANES), BF),
            tail,
            pltpu.SemaphoreType.DMA((3 + PARTS,)),
        ],
        compiler_params=PARAMS,
        name="dispatch_rows",
    )(*(pltpu.with_memory_space_constraint(x, pltpu.HBM) for x in (dy_tokens, routing.T, route_weight.T)))
    got = lax.all_to_all(outgoing, "expert", split_axis=0, concat_axis=0, tiled=True)

    own = lax.axis_index("dp")
    half = hidden_units // 2
    arrived, keep, send, factor = pl.pallas_call(
        functools.partial(partial_kernel, experts, chips),
        out_shape=(
            shape((rows, width), BF),
            shape((half, width), F32),
            shape((half, width), BF),
            shape((rows, 2 * hidden_units), F32),
        ),
        in_specs=[smem, vmem, vmem],
        out_specs=(vmem,) * 4,
        scratch_shapes=[tail],
        compiler_params=PARAMS,
        name="down_partial",
    )(jnp.stack([own // 2, own % 2]), got, pre_act)
    other = lax.ppermute(send, "dp", [(i, i ^ 1) for i in range(replicas)])

    grad_hidden = pl.pallas_call(
        hidden_kernel,
        out_shape=shape((rows, 2 * hidden_units), BF),
        in_specs=[vmem] * 3,
        out_specs=vmem,
        compiler_params=PARAMS,
        name="grad_hidden",
    )(arrived, factor, down_weight)
    other, grad_hidden = lax.optimization_barrier((other, grad_hidden))
    going_back = pl.pallas_call(
        functools.partial(grad_kernel, experts),
        out_shape=pltpu.HBM(block.shape, BF),
        in_specs=[vmem] * 3,
        out_specs=pl.BlockSpec(memory_space=pltpu.HBM),
        scratch_shapes=[
            pltpu.VMEM((experts, block_rows, LANES), BF),
            tail,
            pltpu.SemaphoreType.DMA((PARTS,)),
        ],
        compiler_params=PARAMS,
        name="grad_rows",
    )(grad_hidden, gate_weight, up_weight)
    def pass_on(going, distance):
        hops = [
            (2 * z + c, 2 * ((z + (distance if c == 0 else -distance)) % chips) + c)
            for z in range(chips)
            for c in range(2)
        ]
        return lax.ppermute(going, "dp", hops)

    share = hidden_units // replicas
    count = half // 2
    total = lax.optimization_barrier(keep[:count] + other[:count].astype(F32))
    coming = pass_on((keep[count:] + other[count:].astype(F32)).astype(BF), 1)
    coming, _ = lax.optimization_barrier((coming, going_back))
    count = count // len(NEAR)
    total, *going = [
        total[at : at + count] + coming[at : at + count].astype(F32)
        for at in range(0, half // 2, count)
    ]
    parts = [pass_on(x.astype(BF), move) for x, move in zip(going, NEAR[1:])]
    returned = lax.all_to_all(going_back, "expert", split_axis=0, concat_axis=0, tiled=True)
    piece = (share * width // LANES, LANES)
    own, *going = pl.pallas_call(
        fold_kernel,
        out_shape=(shape(piece, F32),) + (shape(piece, BF),) * 3,
        in_specs=[vmem] * len(NEAR),
        out_specs=(vmem,) * len(FAR),
        scratch_shapes=[pltpu.VMEM((count, width // LANES, LANES), F32)],
        compiler_params=PARAMS,
        name="fold",
    )(total, *parts)
    parts = [pass_on(x, move) for x, move in zip(going, FAR[1:])]
    grad_tokens = pl.pallas_call(
        functools.partial(combine_kernel, experts),
        out_shape=shape((tokens, width), BF),
        in_specs=[vmem] * 2,
        out_specs=vmem,
        scratch_shapes=[tail],
        compiler_params=PARAMS,
        name="combine_rows",
    )(pick, returned)
    parts[0], grad_tokens = lax.optimization_barrier((parts[0], grad_tokens))
    grad_down = pl.pallas_call(
        functools.partial(finish_kernel, 1.0 / replicas),
        out_shape=shape((1, share, width), F32),
        in_specs=[vmem] * len(FAR),
        out_specs=vmem,
        scratch_shapes=[pltpu.VMEM((share, width // LANES, LANES), F32)],
        compiler_params=PARAMS,
        name="finish",
    )(own, *parts)
    return (grad_tokens, grad_down)


def solution(mesh):
    placed = (
        P(("dp", "expert"), None),
        P(("dp", "expert"), None),
        P(("dp", "expert"), None),
        P(("dp", "expert"), None),
        P("expert", None, None),
        P("expert", None, None),
        P("expert", None, None),
    )
    return jax.shard_map(
        per_device,
        mesh=mesh,
        in_specs=placed,
        out_specs=(P(("dp", "expert"), None), P("expert", "dp", None)),
        check_vma=False,
    )
```

```python
import functools

import jax
import jax.numpy as jnp
from jax import lax
from jax.experimental import pallas as pl
from jax.experimental.pallas import tpu as pltpu
from jax.sharding import PartitionSpec as P

BF = jnp.bfloat16
F32 = jnp.float32
LANES = 128
FIRST = 8
PARTS = 4
NEAR = (0, -2, 2, -4)
FAR = (0, 16, 8, -8)
PARAMS = pltpu.CompilerParams(vmem_limit_bytes=16 * 1024 * 1024)


def dot(a, b, contract):
    return lax.dot_general(a, b, (contract, ((), ())), preferred_element_type=F32)


def iota(shape, axis):
    return lax.broadcasted_iota(jnp.int32, shape, axis)


def write_block(ref, tail, pair, first, second, experts):
    main = experts * FIRST
    tiles = [x[:main].reshape(experts, FIRST, LANES) for x in (first, second)]
    ref[:, pair * 16 : pair * 16 + 16, :] = jnp.concatenate(tiles, axis=1).astype(BF)
    tail[:, 2 * pair, :] = first[main:]
    tail[:, 2 * pair + 1, :] = second[main:]


def read_block(ref, tail, pair, experts):
    both = ref[:, pair * 16 : pair * 16 + 16, :].astype(F32)
    main = experts * FIRST
    halves = []
    for at in range(2):
        block = both[:, at * FIRST : (at + 1) * FIRST, :].reshape(main, LANES)
        halves.append(jnp.concatenate([block, tail[:, 2 * pair + at, :]], axis=0))
    return jnp.concatenate(halves, axis=1)


def dispatch_kernel(
    experts, dy_hbm, routing_hbm, weight_hbm, out_ref, pick_ref, dy_ref, routing_ref, weight_ref, tail, sems
):
    loads = [
        pltpu.make_async_copy(source, target, sems.at[i])
        for i, (source, target) in enumerate(
            [(routing_hbm, routing_ref), (weight_hbm, weight_ref), (dy_hbm, dy_ref)]
        )
    ]
    for load in loads:
        load.start()
    loads[0].wait()
    loads[1].wait()
    tokens, width = dy_ref.shape
    route_count = routing_ref.shape[0]
    main = experts * FIRST
    rows = main + experts
    slot = iota((rows, tokens), 0)
    expert = jnp.where(slot < main, slot // FIRST, slot - main)
    position = jnp.where(slot < main, slot % FIRST, FIRST)
    named = jnp.zeros((rows, tokens), F32)
    scale = jnp.zeros((rows, tokens), F32)
    for k in range(route_count):
        hit = routing_ref[k : k + 1, :] == expert
        named = named + jnp.where(hit, 1.0, 0.0)
        scale = scale + jnp.where(hit, weight_ref[k : k + 1, :], 0.0)
    earlier = jnp.where(iota((tokens, tokens), 0) < iota((tokens, tokens), 1), 1.0, 0.0)
    before = dot(named.astype(BF), earlier.astype(BF), ((1,), (0,)))
    pick = jnp.where((named > 0.5) & (before == position.astype(F32)), 1.0, 0.0)
    chosen = pick.astype(BF)
    pick_ref[...] = chosen
    row_weight = jnp.sum(pick * scale, axis=1, keepdims=True)
    loads[2].wait()

    for pair in range(width // (2 * LANES)):
        at = slice(pair * 2 * LANES, (pair + 1) * 2 * LANES)
        part = dot(chosen, dy_ref[:, at], ((1,), (0,))) * row_weight
        write_block(out_ref, tail, pair, part[:, :LANES], part[:, LANES:], experts)
    out_ref[:, experts_rows(width) :, :] = tail[...].astype(BF)


def write_all(columns, width, experts, out_ref, out_hbm, tail, sems):
    pairs = width // (2 * LANES)
    step = pairs // PARTS
    stores = []
    for pair in range(pairs):
        part = columns(slice(pair * 2 * LANES, (pair + 1) * 2 * LANES))
        write_block(out_ref, tail, pair, part[:, :LANES], part[:, LANES:], experts)
        if (pair + 1) % step == 0:
            stop = (pair + 1) * 16
            if pair + 1 == pairs:
                out_ref[:, stop:, :] = tail[...].astype(BF)
                stop = out_ref.shape[1]
            rows = slice(len(stores) * step * 16, stop)
            stores.append(
                pltpu.make_async_copy(
                    out_ref.at[:, rows, :], out_hbm.at[:, rows, :], sems[len(stores)]
                )
            )
            stores[-1].start()
    for store in stores:
        store.wait()


def experts_rows(width):
    return width // LANES * FIRST


def partial_kernel(
    experts, chips, at_ref, got_ref, pre_ref, arrived_ref, keep_ref, send_ref, factor_ref, tail
):
    rows, width = arrived_ref.shape
    hidden_units = pre_ref.shape[1] // 2
    main = experts * FIRST
    capacity = rows // experts
    new, old = iota((rows, rows), 0), iota((rows, rows), 1)
    source = jnp.where(
        new < main, new // FIRST * capacity + new % FIRST, (new - main) * capacity + FIRST
    )
    order = jnp.where(source == old, 1.0, 0.0).astype(BF)
    pre = dot(order, pre_ref[...], ((1,), (0,)))
    gate_pre, up_pre = pre[:, :hidden_units], pre[:, hidden_units:]
    sigmoid = 1.0 / (1.0 + jnp.exp(-gate_pre))
    activated = gate_pre * sigmoid
    factor_ref[:, :hidden_units] = up_pre * sigmoid * (1.0 + gate_pre * (1.0 - sigmoid))
    factor_ref[:, hidden_units:] = activated
    hidden = (activated * up_pre).astype(BF)
    half = hidden_units // 2
    unit, at = iota((hidden_units, hidden_units), 0), iota((hidden_units, hidden_units), 1)
    core = jnp.where(at < half, at_ref[1], 1 - at_ref[1])
    share = half // chips
    place = at % half // share
    far = place // (len(NEAR) * len(FAR))
    for move in range(len(NEAR)):
        far = far + jnp.where(place // len(FAR) % len(NEAR) == move, NEAR[move], 0)
        far = far + jnp.where(place % len(FAR) == move, FAR[move], 0)
    chip = (at_ref[0] + (1 - 2 * core) * far + 2 * chips) % chips
    target = (2 * chip + core) * share + at % share
    hidden = dot(hidden, jnp.where(unit == target, 1.0, 0.0).astype(BF), ((1,), (0,))).astype(BF)
    tail[...] = got_ref[:, experts_rows(width) :, :].astype(F32)
    for pair in range(width // (2 * LANES)):
        at = slice(pair * 2 * LANES, (pair + 1) * 2 * LANES)
        arrived = read_block(got_ref, tail, pair, experts).astype(BF)
        arrived_ref[:, at] = arrived
        part = dot(hidden, arrived, ((0,), (0,)))
        keep_ref[:, at] = part[:half]
        send_ref[:, at] = part[half:].astype(BF)


def hidden_kernel(arrived_ref, factor_ref, down_ref, out_ref):
    grad_hidden = dot(arrived_ref[...], down_ref[0], ((1,), (1,)))
    out_ref[...] = (jnp.concatenate([grad_hidden, grad_hidden], axis=1) * factor_ref[...]).astype(BF)


def grad_kernel(experts, hidden_ref, gate_ref, up_ref, out_hbm, out_ref, tail, sems):
    hidden = hidden_ref[...]

    def columns(at):
        weight = jnp.concatenate([gate_ref[0, at, :], up_ref[0, at, :]], axis=1)
        return dot(hidden, weight, ((1,), (1,)))

    write_all(columns, gate_ref.shape[1], experts, out_ref, out_hbm, tail, [sems.at[i] for i in range(PARTS)])


def combine_kernel(experts, pick_ref, got_ref, out_ref, tail):
    width = out_ref.shape[1]
    tail[...] = got_ref[:, experts_rows(width) :, :].astype(F32)
    pick = pick_ref[...]
    for pair in range(width // (2 * LANES)):
        rows = read_block(got_ref, tail, pair, experts).astype(BF)
        out_ref[:, pair * 2 * LANES : (pair + 1) * 2 * LANES] = dot(
            pick, rows, ((0,), (0,))
        ).astype(BF)


def fold_kernel(total_ref, *refs):
    *coming, own_ref, first_ref, second_ref, third_ref, lines = refs
    for c in range(lines.shape[1]):
        at = slice(c * LANES, (c + 1) * LANES)
        total = total_ref[:, at]
        for ref in coming:
            total = total + ref[:, at].astype(F32)
        lines[:, c, :] = total
    pieces = lines[...].reshape((len(FAR),) + own_ref.shape)
    own_ref[...] = pieces[0]
    first_ref[...] = pieces[1].astype(BF)
    second_ref[...] = pieces[2].astype(BF)
    third_ref[...] = pieces[3].astype(BF)


def finish_kernel(scale, own_ref, *refs):
    *coming, out_ref, lines = refs
    total = own_ref[...]
    for ref in coming:
        total = total + ref[...].astype(F32)
    lines[...] = (total * scale).reshape(lines.shape)
    for c in range(lines.shape[1]):
        out_ref[0, :, c * LANES : (c + 1) * LANES] = lines[:, c, :]


def per_device(dy_tokens, routing, route_weight, pre_act, gate_weight, up_weight, down_weight):
    experts = lax.axis_size("expert")
    replicas = lax.axis_size("dp")
    tokens, width = dy_tokens.shape
    rows = pre_act.shape[0]
    hidden_units = down_weight.shape[1]
    capacity = rows // experts
    assert capacity == FIRST + 1
    block_rows = capacity * width // LANES
    chips = replicas // 2
    assert chips == 2 * len(NEAR) * len(FAR) and hidden_units % replicas == 0
    shape = jax.ShapeDtypeStruct
    vmem = pl.BlockSpec(memory_space=pltpu.VMEM)
    smem = pl.BlockSpec(memory_space=pltpu.SMEM)
    tail = pltpu.VMEM((experts, width // LANES, LANES), F32)
    block = shape((experts, block_rows, LANES), BF)

    outgoing, pick = pl.pallas_call(
        functools.partial(dispatch_kernel, experts),
        out_shape=(block, shape((rows, tokens), BF)),
        in_specs=[pl.BlockSpec(memory_space=pl.ANY)] * 3,
        out_specs=(vmem, vmem),
        scratch_shapes=[
            pltpu.VMEM((tokens, width), BF),
            pltpu.VMEM(routing.T.shape, jnp.int32),
            pltpu.VMEM(route_weight.T.shape, F32),
            tail,
            pltpu.SemaphoreType.DMA((3,)),
        ],
        compiler_params=PARAMS,
        name="dispatch_rows",
    )(*(pltpu.with_memory_space_constraint(x, pltpu.HBM) for x in (dy_tokens, routing.T, route_weight.T)))
    own = lax.axis_index("dp")
    outgoing, place, pre_act = lax.optimization_barrier(
        (outgoing, jnp.stack([own // 2, own % 2]), pre_act)
    )
    got = lax.all_to_all(outgoing, "expert", split_axis=0, concat_axis=0, tiled=True)

    half = hidden_units // 2
    arrived, keep, send, factor = pl.pallas_call(
        functools.partial(partial_kernel, experts, chips),
        out_shape=(
            shape((rows, width), BF),
            shape((half, width), F32),
            shape((half, width), BF),
            shape((rows, 2 * hidden_units), F32),
        ),
        in_specs=[smem, vmem, vmem],
        out_specs=(vmem,) * 4,
        scratch_shapes=[tail],
        compiler_params=PARAMS,
        name="down_partial",
    )(place, got, pre_act)
    other = lax.ppermute(send, "dp", [(i, i ^ 1) for i in range(replicas)])

    grad_hidden = pl.pallas_call(
        hidden_kernel,
        out_shape=shape((rows, 2 * hidden_units), BF),
        in_specs=[vmem] * 3,
        out_specs=vmem,
        compiler_params=PARAMS,
        name="grad_hidden",
    )(arrived, factor, down_weight)
    other, grad_hidden = lax.optimization_barrier((other, grad_hidden))
    going_back = pl.pallas_call(
        functools.partial(grad_kernel, experts),
        out_shape=pltpu.HBM(block.shape, BF),
        in_specs=[vmem] * 3,
        out_specs=pl.BlockSpec(memory_space=pltpu.HBM),
        scratch_shapes=[
            pltpu.VMEM((experts, block_rows, LANES), BF),
            tail,
            pltpu.SemaphoreType.DMA((PARTS,)),
        ],
        compiler_params=PARAMS,
        name="grad_rows",
    )(grad_hidden, gate_weight, up_weight)
    def pass_on(going, distance):
        hops = [
            (2 * z + c, 2 * ((z + (distance if c == 0 else -distance)) % chips) + c)
            for z in range(chips)
            for c in range(2)
        ]
        return lax.ppermute(going, "dp", hops)

    share = hidden_units // replicas
    count = half // 2
    coming = pass_on((keep[count:] + other[count:].astype(F32)).astype(BF), 1)
    keep, other = lax.optimization_barrier((keep, other))
    total = lax.optimization_barrier(keep[:count] + other[:count].astype(F32))
    coming, _ = lax.optimization_barrier((coming, going_back))
    count = count // len(NEAR)
    total, *going = [
        total[at : at + count] + coming[at : at + count].astype(F32)
        for at in range(0, half // 2, count)
    ]
    parts = [pass_on(x.astype(BF), move) for x, move in zip(going, NEAR[1:])]
    returned = lax.all_to_all(going_back, "expert", split_axis=0, concat_axis=0, tiled=True)
    piece = (share * width // LANES, LANES)
    own, *going = pl.pallas_call(
        fold_kernel,
        out_shape=(shape(piece, F32),) + (shape(piece, BF),) * 3,
        in_specs=[vmem] * len(NEAR),
        out_specs=(vmem,) * len(FAR),
        scratch_shapes=[pltpu.VMEM((count, width // LANES, LANES), F32)],
        compiler_params=PARAMS,
        name="fold",
    )(total, *parts)
    parts = [pass_on(x, move) for x, move in zip(going, FAR[1:])]
    grad_tokens = pl.pallas_call(
        functools.partial(combine_kernel, experts),
        out_shape=shape((tokens, width), BF),
        in_specs=[vmem] * 2,
        out_specs=vmem,
        scratch_shapes=[tail],
        compiler_params=PARAMS,
        name="combine_rows",
    )(pick, returned)
    parts[0], grad_tokens = lax.optimization_barrier((parts[0], grad_tokens))
    grad_down = pl.pallas_call(
        functools.partial(finish_kernel, 1.0 / replicas),
        out_shape=shape((1, share, width), F32),
        in_specs=[vmem] * len(FAR),
        out_specs=vmem,
        scratch_shapes=[pltpu.VMEM((share, width // LANES, LANES), F32)],
        compiler_params=PARAMS,
        name="finish",
    )(own, *parts)
    return (grad_tokens, grad_down)


def solution(mesh):
    placed = (
        P(("dp", "expert"), None),
        P(("dp", "expert"), None),
        P(("dp", "expert"), None),
        P(("dp", "expert"), None),
        P("expert", None, None),
        P("expert", None, None),
        P("expert", None, None),
    )
    return jax.shard_map(
        per_device,
        mesh=mesh,
        in_specs=placed,
        out_specs=(P(("dp", "expert"), None), P("expert", "dp", None)),
        check_vma=False,
    )
```

```python
import functools

import jax
import jax.numpy as jnp
from jax import lax
from jax.experimental import pallas as pl
from jax.experimental.pallas import tpu as pltpu
from jax.sharding import PartitionSpec as P

BF = jnp.bfloat16
F32 = jnp.float32
LANES = 128
FIRST = 8
PARTS = 4
NEAR = (0, -2, 2, -4)
FAR = (0, 16, -8, 8)
PARAMS = pltpu.CompilerParams(vmem_limit_bytes=16 * 1024 * 1024)


def dot(a, b, contract):
    return lax.dot_general(a, b, (contract, ((), ())), preferred_element_type=F32)


def iota(shape, axis):
    return lax.broadcasted_iota(jnp.int32, shape, axis)


def write_block(ref, tail, pair, first, second, experts):
    main = experts * FIRST
    tiles = [x[:main].reshape(experts, FIRST, LANES) for x in (first, second)]
    ref[:, pair * 16 : pair * 16 + 16, :] = jnp.concatenate(tiles, axis=1).astype(BF)
    tail[:, 2 * pair, :] = first[main:]
    tail[:, 2 * pair + 1, :] = second[main:]


def read_block(ref, tail, pair, experts):
    both = ref[:, pair * 16 : pair * 16 + 16, :].astype(F32)
    main = experts * FIRST
    halves = []
    for at in range(2):
        block = both[:, at * FIRST : (at + 1) * FIRST, :].reshape(main, LANES)
        halves.append(jnp.concatenate([block, tail[:, 2 * pair + at, :]], axis=0))
    return jnp.concatenate(halves, axis=1)


def dispatch_kernel(
    experts, dy_hbm, routing_hbm, weight_hbm, out_ref, pick_ref, dy_ref, routing_ref, weight_ref, tail, sems
):
    loads = [
        pltpu.make_async_copy(source, target, sems.at[i])
        for i, (source, target) in enumerate(
            [(routing_hbm, routing_ref), (weight_hbm, weight_ref), (dy_hbm, dy_ref)]
        )
    ]
    for load in loads:
        load.start()
    loads[0].wait()
    loads[1].wait()
    tokens, width = dy_ref.shape
    route_count = routing_ref.shape[0]
    main = experts * FIRST
    rows = main + experts
    slot = iota((rows, tokens), 0)
    expert = jnp.where(slot < main, slot // FIRST, slot - main)
    position = jnp.where(slot < main, slot % FIRST, FIRST)
    named = jnp.zeros((rows, tokens), F32)
    scale = jnp.zeros((rows, tokens), F32)
    for k in range(route_count):
        hit = routing_ref[k : k + 1, :] == expert
        named = named + jnp.where(hit, 1.0, 0.0)
        scale = scale + jnp.where(hit, weight_ref[k : k + 1, :], 0.0)
    earlier = jnp.where(iota((tokens, tokens), 0) < iota((tokens, tokens), 1), 1.0, 0.0)
    before = dot(named.astype(BF), earlier.astype(BF), ((1,), (0,)))
    pick = jnp.where((named > 0.5) & (before == position.astype(F32)), 1.0, 0.0)
    chosen = pick.astype(BF)
    pick_ref[...] = chosen
    row_weight = jnp.sum(pick * scale, axis=1, keepdims=True)
    loads[2].wait()

    for pair in range(width // (2 * LANES)):
        at = slice(pair * 2 * LANES, (pair + 1) * 2 * LANES)
        part = dot(chosen, dy_ref[:, at], ((1,), (0,))) * row_weight
        write_block(out_ref, tail, pair, part[:, :LANES], part[:, LANES:], experts)
    out_ref[:, experts_rows(width) :, :] = tail[...].astype(BF)


def write_all(columns, width, experts, out_ref, out_hbm, tail, sems):
    pairs = width // (2 * LANES)
    step = pairs // PARTS
    stores = []
    for pair in range(pairs):
        part = columns(slice(pair * 2 * LANES, (pair + 1) * 2 * LANES))
        write_block(out_ref, tail, pair, part[:, :LANES], part[:, LANES:], experts)
        if (pair + 1) % step == 0:
            stop = (pair + 1) * 16
            if pair + 1 == pairs:
                out_ref[:, stop:, :] = tail[...].astype(BF)
                stop = out_ref.shape[1]
            rows = slice(len(stores) * step * 16, stop)
            stores.append(
                pltpu.make_async_copy(
                    out_ref.at[:, rows, :], out_hbm.at[:, rows, :], sems[len(stores)]
                )
            )
            stores[-1].start()
    for store in stores:
        store.wait()


def experts_rows(width):
    return width // LANES * FIRST


def partial_kernel(
    experts, chips, at_ref, got_ref, pre_ref, arrived_ref, keep_ref, send_ref, factor_ref, tail
):
    rows, width = arrived_ref.shape
    hidden_units = pre_ref.shape[1] // 2
    main = experts * FIRST
    capacity = rows // experts
    new, old = iota((rows, rows), 0), iota((rows, rows), 1)
    source = jnp.where(
        new < main, new // FIRST * capacity + new % FIRST, (new - main) * capacity + FIRST
    )
    order = jnp.where(source == old, 1.0, 0.0).astype(BF)
    pre = dot(order, pre_ref[...], ((1,), (0,)))
    gate_pre, up_pre = pre[:, :hidden_units], pre[:, hidden_units:]
    sigmoid = 1.0 / (1.0 + jnp.exp(-gate_pre))
    activated = gate_pre * sigmoid
    factor_ref[:, :hidden_units] = up_pre * sigmoid * (1.0 + gate_pre * (1.0 - sigmoid))
    factor_ref[:, hidden_units:] = activated
    hidden = (activated * up_pre).astype(BF)
    half = hidden_units // 2
    unit, at = iota((hidden_units, hidden_units), 0), iota((hidden_units, hidden_units), 1)
    core = jnp.where(at < half, at_ref[1], 1 - at_ref[1])
    share = half // chips
    place = at % half // share
    sign = 1 - 2 * core
    far = place // (len(NEAR) * len(FAR)) * sign
    for move in range(len(NEAR)):
        far = far + jnp.where(place // len(FAR) % len(NEAR) == move, NEAR[move], 0) * sign
        far = far + jnp.where(place % len(FAR) == move, FAR[move], 0)
    chip = (at_ref[0] + far + 2 * chips) % chips
    target = (2 * chip + core) * share + at % share
    hidden = dot(hidden, jnp.where(unit == target, 1.0, 0.0).astype(BF), ((1,), (0,))).astype(BF)
    tail[...] = got_ref[:, experts_rows(width) :, :].astype(F32)
    for pair in range(width // (2 * LANES)):
        at = slice(pair * 2 * LANES, (pair + 1) * 2 * LANES)
        arrived = read_block(got_ref, tail, pair, experts).astype(BF)
        arrived_ref[:, at] = arrived
        part = dot(hidden, arrived, ((0,), (0,)))
        keep_ref[:, at] = part[:half]
        send_ref[:, at] = part[half:].astype(BF)


def hidden_kernel(arrived_ref, factor_ref, down_ref, out_ref):
    grad_hidden = dot(arrived_ref[...], down_ref[0], ((1,), (1,)))
    out_ref[...] = (jnp.concatenate([grad_hidden, grad_hidden], axis=1) * factor_ref[...]).astype(BF)


def grad_kernel(experts, hidden_ref, gate_ref, up_ref, out_hbm, out_ref, tail, sems):
    hidden = hidden_ref[...]

    def columns(at):
        weight = jnp.concatenate([gate_ref[0, at, :], up_ref[0, at, :]], axis=1)
        return dot(hidden, weight, ((1,), (1,)))

    write_all(columns, gate_ref.shape[1], experts, out_ref, out_hbm, tail, [sems.at[i] for i in range(PARTS)])


def combine_kernel(experts, pick_ref, got_ref, out_ref, tail):
    width = out_ref.shape[1]
    tail[...] = got_ref[:, experts_rows(width) :, :].astype(F32)
    pick = pick_ref[...]
    for pair in range(width // (2 * LANES)):
        rows = read_block(got_ref, tail, pair, experts).astype(BF)
        out_ref[:, pair * 2 * LANES : (pair + 1) * 2 * LANES] = dot(
            pick, rows, ((0,), (0,))
        ).astype(BF)


def fold_kernel(total_ref, *refs):
    *coming, own_ref, first_ref, second_ref, third_ref, lines = refs
    for c in range(lines.shape[1]):
        at = slice(c * LANES, (c + 1) * LANES)
        total = total_ref[:, at]
        for ref in coming:
            total = total + ref[:, at].astype(F32)
        lines[:, c, :] = total
    pieces = lines[...].reshape((len(FAR),) + own_ref.shape)
    own_ref[...] = pieces[0]
    first_ref[...] = pieces[1].astype(BF)
    second_ref[...] = pieces[2].astype(BF)
    third_ref[...] = pieces[3].astype(BF)


def finish_kernel(scale, own_ref, *refs):
    *coming, out_ref, lines = refs
    total = own_ref[...]
    for ref in coming:
        total = total + ref[...].astype(F32)
    lines[...] = (total * scale).reshape(lines.shape)
    for c in range(lines.shape[1]):
        out_ref[0, :, c * LANES : (c + 1) * LANES] = lines[:, c, :]


def per_device(dy_tokens, routing, route_weight, pre_act, gate_weight, up_weight, down_weight):
    experts = lax.axis_size("expert")
    replicas = lax.axis_size("dp")
    tokens, width = dy_tokens.shape
    rows = pre_act.shape[0]
    hidden_units = down_weight.shape[1]
    capacity = rows // experts
    assert capacity == FIRST + 1
    block_rows = capacity * width // LANES
    chips = replicas // 2
    assert chips == 2 * len(NEAR) * len(FAR) and hidden_units % replicas == 0
    shape = jax.ShapeDtypeStruct
    vmem = pl.BlockSpec(memory_space=pltpu.VMEM)
    smem = pl.BlockSpec(memory_space=pltpu.SMEM)
    tail = pltpu.VMEM((experts, width // LANES, LANES), F32)
    block = shape((experts, block_rows, LANES), BF)

    outgoing, pick = pl.pallas_call(
        functools.partial(dispatch_kernel, experts),
        out_shape=(block, shape((rows, tokens), BF)),
        in_specs=[pl.BlockSpec(memory_space=pl.ANY)] * 3,
        out_specs=(vmem, vmem),
        scratch_shapes=[
            pltpu.VMEM((tokens, width), BF),
            pltpu.VMEM(routing.T.shape, jnp.int32),
            pltpu.VMEM(route_weight.T.shape, F32),
            tail,
            pltpu.SemaphoreType.DMA((3,)),
        ],
        compiler_params=PARAMS,
        name="dispatch_rows",
    )(*(pltpu.with_memory_space_constraint(x, pltpu.HBM) for x in (dy_tokens, routing.T, route_weight.T)))
    own = lax.axis_index("dp")
    outgoing, place, pre_act = lax.optimization_barrier(
        (outgoing, jnp.stack([own // 2, own % 2]), pre_act)
    )
    got = lax.all_to_all(outgoing, "expert", split_axis=0, concat_axis=0, tiled=True)

    half = hidden_units // 2
    arrived, keep, send, factor = pl.pallas_call(
        functools.partial(partial_kernel, experts, chips),
        out_shape=(
            shape((rows, width), BF),
            shape((half, width), F32),
            shape((half, width), BF),
            shape((rows, 2 * hidden_units), F32),
        ),
        in_specs=[smem, vmem, vmem],
        out_specs=(vmem,) * 4,
        scratch_shapes=[tail],
        compiler_params=PARAMS,
        name="down_partial",
    )(place, got, pre_act)
    other = lax.ppermute(send, "dp", [(i, i ^ 1) for i in range(replicas)])

    grad_hidden = pl.pallas_call(
        hidden_kernel,
        out_shape=shape((rows, 2 * hidden_units), BF),
        in_specs=[vmem] * 3,
        out_specs=vmem,
        compiler_params=PARAMS,
        name="grad_hidden",
    )(arrived, factor, down_weight)
    going_back = pl.pallas_call(
        functools.partial(grad_kernel, experts),
        out_shape=pltpu.HBM(block.shape, BF),
        in_specs=[vmem] * 3,
        out_specs=pl.BlockSpec(memory_space=pltpu.HBM),
        scratch_shapes=[
            pltpu.VMEM((experts, block_rows, LANES), BF),
            tail,
            pltpu.SemaphoreType.DMA((PARTS,)),
        ],
        compiler_params=PARAMS,
        name="grad_rows",
    )(grad_hidden, gate_weight, up_weight)
    def pass_on(going, moves):
        hops = [(2 * z + c, 2 * ((z + moves[c]) % chips) + c) for z in range(chips) for c in range(2)]
        return lax.ppermute(going, "dp", hops)

    share = hidden_units // replicas
    count = half // 2
    other, _ = lax.optimization_barrier((other, going_back))
    total = lax.optimization_barrier(keep[:count] + other[:count].astype(F32))
    going = (keep[count:] + other[count:].astype(F32)).astype(BF)
    going, going_back = lax.optimization_barrier((going, going_back))
    coming = pass_on(going, (1, -1))
    count = count // len(NEAR)
    total, *going = [
        total[at : at + count] + coming[at : at + count].astype(F32)
        for at in range(0, half // 2, count)
    ]
    parts = [pass_on(x.astype(BF), (move, -move)) for x, move in zip(going, NEAR[1:])]
    returned = lax.all_to_all(going_back, "expert", split_axis=0, concat_axis=0, tiled=True)
    piece = (share * width // LANES, LANES)
    own, *going = pl.pallas_call(
        fold_kernel,
        out_shape=(shape(piece, F32),) + (shape(piece, BF),) * 3,
        in_specs=[vmem] * len(NEAR),
        out_specs=(vmem,) * len(FAR),
        scratch_shapes=[pltpu.VMEM((count, width // LANES, LANES), F32)],
        compiler_params=PARAMS,
        name="fold",
    )(total, *parts)
    parts = [pass_on(x, (move, move)) for x, move in zip(going, FAR[1:])]
    grad_tokens = pl.pallas_call(
        functools.partial(combine_kernel, experts),
        out_shape=shape((tokens, width), BF),
        in_specs=[vmem] * 2,
        out_specs=vmem,
        scratch_shapes=[tail],
        compiler_params=PARAMS,
        name="combine_rows",
    )(pick, returned)
    parts[0], grad_tokens = lax.optimization_barrier((parts[0], grad_tokens))
    grad_down = pl.pallas_call(
        functools.partial(finish_kernel, 1.0 / replicas),
        out_shape=shape((1, share, width), F32),
        in_specs=[vmem] * len(FAR),
        out_specs=vmem,
        scratch_shapes=[pltpu.VMEM((share, width // LANES, LANES), F32)],
        compiler_params=PARAMS,
        name="finish",
    )(own, *parts)
    return (grad_tokens, grad_down)


def solution(mesh):
    placed = (
        P(("dp", "expert"), None),
        P(("dp", "expert"), None),
        P(("dp", "expert"), None),
        P(("dp", "expert"), None),
        P("expert", None, None),
        P("expert", None, None),
        P("expert", None, None),
    )
    return jax.shard_map(
        per_device,
        mesh=mesh,
        in_specs=placed,
        out_specs=(P(("dp", "expert"), None), P("expert", "dp", None)),
        check_vma=False,
    )
```

```python
import functools

import jax
import jax.numpy as jnp
from jax import lax
from jax.experimental import pallas as pl
from jax.experimental.pallas import tpu as pltpu
from jax.sharding import PartitionSpec as P

BF = jnp.bfloat16
F32 = jnp.float32
LANES = 128
FIRST = 8
PARTS = 4
NEAR = (0, -2, 2, -4)
FAR = (0, 16, -8, 8)
PARAMS = pltpu.CompilerParams(vmem_limit_bytes=16 * 1024 * 1024)


def dot(a, b, contract):
    return lax.dot_general(a, b, (contract, ((), ())), preferred_element_type=F32)


def iota(shape, axis):
    return lax.broadcasted_iota(jnp.int32, shape, axis)


def write_block(ref, tail, pair, first, second, experts):
    main = experts * FIRST
    tiles = [x[:main].reshape(experts, FIRST, LANES) for x in (first, second)]
    ref[:, pair * 16 : pair * 16 + 16, :] = jnp.concatenate(tiles, axis=1).astype(BF)
    tail[:, 2 * pair, :] = first[main:]
    tail[:, 2 * pair + 1, :] = second[main:]


def read_block(ref, tail, pair, experts):
    both = ref[:, pair * 16 : pair * 16 + 16, :].astype(F32)
    main = experts * FIRST
    halves = []
    for at in range(2):
        block = both[:, at * FIRST : (at + 1) * FIRST, :].reshape(main, LANES)
        halves.append(jnp.concatenate([block, tail[:, 2 * pair + at, :]], axis=0))
    return jnp.concatenate(halves, axis=1)


def dispatch_kernel(
    experts, dy_hbm, routing_hbm, weight_hbm, out_ref, pick_ref, dy_ref, routing_ref, weight_ref, tail, sems
):
    loads = [
        pltpu.make_async_copy(source, target, sems.at[i])
        for i, (source, target) in enumerate(
            [(routing_hbm, routing_ref), (weight_hbm, weight_ref), (dy_hbm, dy_ref)]
        )
    ]
    for load in loads:
        load.start()
    loads[0].wait()
    loads[1].wait()
    tokens, width = dy_ref.shape
    route_count = routing_ref.shape[0]
    main = experts * FIRST
    rows = main + experts
    slot = iota((rows, tokens), 0)
    expert = jnp.where(slot < main, slot >> 3, slot - main)
    position = jnp.where(slot < main, slot & (FIRST - 1), FIRST)
    named = jnp.zeros((rows, tokens), F32)
    scale = jnp.zeros((rows, tokens), F32)
    for k in range(route_count):
        hit = routing_ref[k : k + 1, :] == expert
        named = named + jnp.where(hit, 1.0, 0.0)
        scale = scale + jnp.where(hit, weight_ref[k : k + 1, :], 0.0)
    earlier = jnp.where(iota((tokens, tokens), 0) < iota((tokens, tokens), 1), 1.0, 0.0)
    before = dot(named.astype(BF), earlier.astype(BF), ((1,), (0,)))
    pick = jnp.where((named > 0.5) & (before == position.astype(F32)), 1.0, 0.0)
    chosen = pick.astype(BF)
    pick_ref[...] = chosen
    row_weight = jnp.sum(pick * scale, axis=1, keepdims=True)
    loads[2].wait()

    for pair in range(width // (2 * LANES)):
        at = slice(pair * 2 * LANES, (pair + 1) * 2 * LANES)
        part = dot(chosen, dy_ref[:, at], ((1,), (0,))) * row_weight
        write_block(out_ref, tail, pair, part[:, :LANES], part[:, LANES:], experts)
    out_ref[:, experts_rows(width) :, :] = tail[...].astype(BF)


def write_all(columns, width, experts, out_ref, out_hbm, tail, sems):
    pairs = width // (2 * LANES)
    step = pairs // PARTS
    stores = []
    for pair in range(pairs):
        part = columns(slice(pair * 2 * LANES, (pair + 1) * 2 * LANES))
        write_block(out_ref, tail, pair, part[:, :LANES], part[:, LANES:], experts)
        if (pair + 1) % step == 0:
            stop = (pair + 1) * 16
            if pair + 1 == pairs:
                out_ref[:, stop:, :] = tail[...].astype(BF)
                stop = out_ref.shape[1]
            rows = slice(len(stores) * step * 16, stop)
            stores.append(
                pltpu.make_async_copy(
                    out_ref.at[:, rows, :], out_hbm.at[:, rows, :], sems[len(stores)]
                )
            )
            stores[-1].start()
    for store in stores:
        store.wait()


def experts_rows(width):
    return width // LANES * FIRST


def partial_kernel(
    experts, chips, at_ref, got_ref, pre_ref, arrived_ref, keep_ref, send_ref, factor_ref, tail
):
    rows, width = arrived_ref.shape
    hidden_units = pre_ref.shape[1] // 2
    main = experts * FIRST
    capacity = rows // experts
    new, old = iota((rows, rows), 0), iota((rows, rows), 1)
    source = jnp.where(
        new < main, (new >> 3) * capacity + (new & (FIRST - 1)), (new - main) * capacity + FIRST
    )
    order = jnp.where(source == old, 1.0, 0.0).astype(BF)
    pre = dot(order, pre_ref[...], ((1,), (0,)))
    gate_pre, up_pre = pre[:, :hidden_units], pre[:, hidden_units:]
    sigmoid = 1.0 / (1.0 + jnp.exp(-gate_pre))
    activated = gate_pre * sigmoid
    factor_ref[:, :hidden_units] = up_pre * sigmoid * (1.0 + gate_pre * (1.0 - sigmoid))
    factor_ref[:, hidden_units:] = activated
    hidden = (activated * up_pre).astype(BF)
    half = hidden_units // 2
    unit, at = iota((hidden_units, hidden_units), 0), iota((hidden_units, hidden_units), 1)
    core = jnp.where(at < half, at_ref[1], 1 - at_ref[1])
    share = half // chips
    place = (at & (half - 1)) >> 1
    sign = 1 - 2 * core
    far = jnp.zeros_like(place)
    near = jnp.where(place >= len(NEAR) * len(FAR), 1, 0)
    for move in range(1, len(NEAR)):
        near = near + jnp.where((place >> 2) & 3 == move, NEAR[move], 0)
        far = far + jnp.where(place & 3 == move, FAR[move], 0)
    chip = (at_ref[0] + near * sign + far) & (chips - 1)
    target = (2 * chip + core) * share + (at & 1)
    hidden = dot(hidden, jnp.where(unit == target, 1.0, 0.0).astype(BF), ((1,), (0,))).astype(BF)
    tail[...] = got_ref[:, experts_rows(width) :, :].astype(F32)
    for pair in range(width // (2 * LANES)):
        at = slice(pair * 2 * LANES, (pair + 1) * 2 * LANES)
        arrived = read_block(got_ref, tail, pair, experts).astype(BF)
        arrived_ref[:, at] = arrived
        part = dot(hidden, arrived, ((0,), (0,)))
        keep_ref[:, at] = part[:half]
        send_ref[:, at] = part[half:].astype(BF)


def hidden_kernel(arrived_ref, factor_ref, down_ref, out_ref):
    grad_hidden = dot(arrived_ref[...], down_ref[0], ((1,), (1,)))
    out_ref[...] = (jnp.concatenate([grad_hidden, grad_hidden], axis=1) * factor_ref[...]).astype(BF)


def grad_kernel(experts, hidden_ref, gate_ref, up_ref, out_hbm, out_ref, tail, sems):
    hidden = hidden_ref[...]

    def columns(at):
        weight = jnp.concatenate([gate_ref[0, at, :], up_ref[0, at, :]], axis=1)
        return dot(hidden, weight, ((1,), (1,)))

    write_all(columns, gate_ref.shape[1], experts, out_ref, out_hbm, tail, [sems.at[i] for i in range(PARTS)])


def combine_kernel(experts, pick_ref, got_ref, out_ref, tail):
    width = out_ref.shape[1]
    tail[...] = got_ref[:, experts_rows(width) :, :].astype(F32)
    pick = pick_ref[...]
    for pair in range(width // (2 * LANES)):
        rows = read_block(got_ref, tail, pair, experts).astype(BF)
        out_ref[:, pair * 2 * LANES : (pair + 1) * 2 * LANES] = dot(
            pick, rows, ((0,), (0,))
        ).astype(BF)


def fold_kernel(total_ref, *refs):
    *coming, own_ref, first_ref, second_ref, third_ref, lines = refs
    for c in range(lines.shape[1]):
        at = slice(c * LANES, (c + 1) * LANES)
        total = total_ref[:, at]
        for ref in coming:
            total = total + ref[:, at].astype(F32)
        lines[:, c, :] = total
    pieces = lines[...].reshape((len(FAR),) + own_ref.shape)
    own_ref[...] = pieces[0]
    first_ref[...] = pieces[1].astype(BF)
    second_ref[...] = pieces[2].astype(BF)
    third_ref[...] = pieces[3].astype(BF)


def finish_kernel(scale, own_ref, *refs):
    *coming, out_ref, lines = refs
    total = own_ref[...]
    for ref in coming:
        total = total + ref[...].astype(F32)
    lines[...] = (total * scale).reshape(lines.shape)
    for c in range(lines.shape[1]):
        out_ref[0, :, c * LANES : (c + 1) * LANES] = lines[:, c, :]


def per_device(dy_tokens, routing, route_weight, pre_act, gate_weight, up_weight, down_weight):
    experts = lax.axis_size("expert")
    replicas = lax.axis_size("dp")
    tokens, width = dy_tokens.shape
    rows = pre_act.shape[0]
    hidden_units = down_weight.shape[1]
    capacity = rows // experts
    assert capacity == FIRST + 1
    block_rows = capacity * width // LANES
    chips = replicas // 2
    assert chips == 2 * len(NEAR) * len(FAR) and hidden_units == 2 * replicas and FIRST == 8
    shape = jax.ShapeDtypeStruct
    vmem = pl.BlockSpec(memory_space=pltpu.VMEM)
    smem = pl.BlockSpec(memory_space=pltpu.SMEM)
    tail = pltpu.VMEM((experts, width // LANES, LANES), F32)
    block = shape((experts, block_rows, LANES), BF)

    outgoing, pick = pl.pallas_call(
        functools.partial(dispatch_kernel, experts),
        out_shape=(block, shape((rows, tokens), BF)),
        in_specs=[pl.BlockSpec(memory_space=pl.ANY)] * 3,
        out_specs=(vmem, vmem),
        scratch_shapes=[
            pltpu.VMEM((tokens, width), BF),
            pltpu.VMEM(routing.T.shape, jnp.int32),
            pltpu.VMEM(route_weight.T.shape, F32),
            tail,
            pltpu.SemaphoreType.DMA((3,)),
        ],
        compiler_params=PARAMS,
        name="dispatch_rows",
    )(*(pltpu.with_memory_space_constraint(x, pltpu.HBM) for x in (dy_tokens, routing.T, route_weight.T)))
    own = lax.axis_index("dp")
    outgoing, place, pre_act = lax.optimization_barrier(
        (outgoing, jnp.stack([own // 2, own % 2]), pre_act)
    )
    got = lax.all_to_all(outgoing, "expert", split_axis=0, concat_axis=0, tiled=True)

    half = hidden_units // 2
    arrived, keep, send, factor = pl.pallas_call(
        functools.partial(partial_kernel, experts, chips),
        out_shape=(
            shape((rows, width), BF),
            shape((half, width), F32),
            shape((half, width), BF),
            shape((rows, 2 * hidden_units), F32),
        ),
        in_specs=[smem, vmem, vmem],
        out_specs=(vmem,) * 4,
        scratch_shapes=[tail],
        compiler_params=PARAMS,
        name="down_partial",
    )(place, got, pre_act)
    other = lax.ppermute(send, "dp", [(i, i ^ 1) for i in range(replicas)])

    grad_hidden = pl.pallas_call(
        hidden_kernel,
        out_shape=shape((rows, 2 * hidden_units), BF),
        in_specs=[vmem] * 3,
        out_specs=vmem,
        compiler_params=PARAMS,
        name="grad_hidden",
    )(arrived, factor, down_weight)
    going_back = pl.pallas_call(
        functools.partial(grad_kernel, experts),
        out_shape=pltpu.HBM(block.shape, BF),
        in_specs=[vmem] * 3,
        out_specs=pl.BlockSpec(memory_space=pltpu.HBM),
        scratch_shapes=[
            pltpu.VMEM((experts, block_rows, LANES), BF),
            tail,
            pltpu.SemaphoreType.DMA((PARTS,)),
        ],
        compiler_params=PARAMS,
        name="grad_rows",
    )(grad_hidden, gate_weight, up_weight)
    def pass_on(going, moves):
        hops = [(2 * z + c, 2 * ((z + moves[c]) % chips) + c) for z in range(chips) for c in range(2)]
        return lax.ppermute(going, "dp", hops)

    share = hidden_units // replicas
    count = half // 2
    other, _ = lax.optimization_barrier((other, going_back))
    total = lax.optimization_barrier(keep[:count] + other[:count].astype(F32))
    going = (keep[count:] + other[count:].astype(F32)).astype(BF)
    going, going_back = lax.optimization_barrier((going, going_back))
    coming = pass_on(going, (1, -1))
    count = count // len(NEAR)
    total, *going = [
        total[at : at + count] + coming[at : at + count].astype(F32)
        for at in range(0, half // 2, count)
    ]
    parts = [pass_on(x.astype(BF), (move, -move)) for x, move in zip(going, NEAR[1:])]
    returned = lax.all_to_all(going_back, "expert", split_axis=0, concat_axis=0, tiled=True)
    piece = (share * width // LANES, LANES)
    own, *going = pl.pallas_call(
        fold_kernel,
        out_shape=(shape(piece, F32),) + (shape(piece, BF),) * 3,
        in_specs=[vmem] * len(NEAR),
        out_specs=(vmem,) * len(FAR),
        scratch_shapes=[pltpu.VMEM((count, width // LANES, LANES), F32)],
        compiler_params=PARAMS,
        name="fold",
    )(total, *parts)
    parts = [pass_on(x, (move, move)) for x, move in zip(going, FAR[1:])]
    grad_tokens = pl.pallas_call(
        functools.partial(combine_kernel, experts),
        out_shape=shape((tokens, width), BF),
        in_specs=[vmem] * 2,
        out_specs=vmem,
        scratch_shapes=[tail],
        compiler_params=PARAMS,
        name="combine_rows",
    )(pick, returned)
    parts[0], grad_tokens = lax.optimization_barrier((parts[0], grad_tokens))
    grad_down = pl.pallas_call(
        functools.partial(finish_kernel, 1.0 / replicas),
        out_shape=shape((1, share, width), F32),
        in_specs=[vmem] * len(FAR),
        out_specs=vmem,
        scratch_shapes=[pltpu.VMEM((share, width // LANES, LANES), F32)],
        compiler_params=PARAMS,
        name="finish",
    )(own, *parts)
    return (grad_tokens, grad_down)


def solution(mesh):
    placed = (
        P(("dp", "expert"), None),
        P(("dp", "expert"), None),
        P(("dp", "expert"), None),
        P(("dp", "expert"), None),
        P("expert", None, None),
        P("expert", None, None),
        P("expert", None, None),
    )
    return jax.shard_map(
        per_device,
        mesh=mesh,
        in_specs=placed,
        out_specs=(P(("dp", "expert"), None), P("expert", "dp", None)),
        check_vma=False,
    )
```

```python
import functools

import jax
import jax.numpy as jnp
from jax import lax
from jax.experimental import pallas as pl
from jax.experimental.pallas import tpu as pltpu
from jax.sharding import PartitionSpec as P

BF = jnp.bfloat16
F32 = jnp.float32
LANES = 128
FIRST = 8
PARTS = 4
NEAR = (0, -2, 2, -4)
FAR = (0, 16, -8, 8)
PARAMS = pltpu.CompilerParams(vmem_limit_bytes=16 * 1024 * 1024)


def dot(a, b, contract):
    return lax.dot_general(a, b, (contract, ((), ())), preferred_element_type=F32)


def iota(shape, axis):
    return lax.broadcasted_iota(jnp.int32, shape, axis)


def write_block(ref, tail, pair, first, second, experts):
    main = experts * FIRST
    tiles = [x[:main].reshape(experts, FIRST, LANES) for x in (first, second)]
    ref[:, pair * 16 : pair * 16 + 16, :] = jnp.concatenate(tiles, axis=1).astype(BF)
    tail[:, 2 * pair, :] = first[main:]
    tail[:, 2 * pair + 1, :] = second[main:]


def read_block(ref, tail, pair, experts):
    both = ref[:, pair * 16 : pair * 16 + 16, :].astype(F32)
    main = experts * FIRST
    halves = []
    for at in range(2):
        block = both[:, at * FIRST : (at + 1) * FIRST, :].reshape(main, LANES)
        halves.append(jnp.concatenate([block, tail[:, 2 * pair + at, :]], axis=0))
    return jnp.concatenate(halves, axis=1)


def dispatch_kernel(
    experts, dy_hbm, routing_hbm, weight_hbm, out_ref, pick_ref, dy_ref, routing_ref, weight_ref, tail, sems
):
    loads = [
        pltpu.make_async_copy(source, target, sems.at[i])
        for i, (source, target) in enumerate(
            [(routing_hbm, routing_ref), (weight_hbm, weight_ref), (dy_hbm, dy_ref)]
        )
    ]
    for load in loads:
        load.start()
    loads[0].wait()
    loads[1].wait()
    tokens, width = dy_ref.shape
    route_count = routing_ref.shape[0]
    main = experts * FIRST
    rows = main + experts
    slot = iota((rows, tokens), 0)
    expert = jnp.where(slot < main, slot >> 3, slot - main)
    position = jnp.where(slot < main, slot & (FIRST - 1), FIRST)
    named = jnp.zeros((rows, tokens), F32)
    scale = jnp.zeros((rows, tokens), F32)
    for k in range(route_count):
        hit = routing_ref[k : k + 1, :] == expert
        named = named + jnp.where(hit, 1.0, 0.0)
        scale = scale + jnp.where(hit, weight_ref[k : k + 1, :], 0.0)
    earlier = jnp.where(iota((tokens, tokens), 0) < iota((tokens, tokens), 1), 1.0, 0.0)
    before = dot(named.astype(BF), earlier.astype(BF), ((1,), (0,)))
    pick = jnp.where((named > 0.5) & (before == position.astype(F32)), 1.0, 0.0)
    chosen = pick.astype(BF)
    pick_ref[...] = chosen
    row_weight = jnp.sum(pick * scale, axis=1, keepdims=True)
    loads[2].wait()

    for pair in range(width // (2 * LANES)):
        at = slice(pair * 2 * LANES, (pair + 1) * 2 * LANES)
        part = dot(chosen, dy_ref[:, at], ((1,), (0,))) * row_weight
        write_block(out_ref, tail, pair, part[:, :LANES], part[:, LANES:], experts)
    out_ref[:, experts_rows(width) :, :] = tail[...].astype(BF)


def write_all(columns, width, experts, out_ref, out_hbm, tail, sems):
    pairs = width // (2 * LANES)
    step = pairs // PARTS
    stores = []
    for pair in range(pairs):
        part = columns(slice(pair * 2 * LANES, (pair + 1) * 2 * LANES))
        write_block(out_ref, tail, pair, part[:, :LANES], part[:, LANES:], experts)
        if (pair + 1) % step == 0:
            stop = (pair + 1) * 16
            if pair + 1 == pairs:
                out_ref[:, stop:, :] = tail[...].astype(BF)
                stop = out_ref.shape[1]
            rows = slice(len(stores) * step * 16, stop)
            stores.append(
                pltpu.make_async_copy(
                    out_ref.at[:, rows, :], out_hbm.at[:, rows, :], sems[len(stores)]
                )
            )
            stores[-1].start()
    for store in stores:
        store.wait()


def experts_rows(width):
    return width // LANES * FIRST


def partial_kernel(
    experts, chips, at_ref, got_ref, pre_ref, arrived_ref, own_ref, send_ref, factor_ref, tail
):
    rows, width = arrived_ref.shape
    hidden_units = pre_ref.shape[1] // 2
    main = experts * FIRST
    capacity = rows // experts
    new, old = iota((rows, rows), 0), iota((rows, rows), 1)
    source = jnp.where(
        new < main, (new >> 3) * capacity + (new & (FIRST - 1)), (new - main) * capacity + FIRST
    )
    order = jnp.where(source == old, 1.0, 0.0).astype(BF)
    pre = dot(order, pre_ref[...], ((1,), (0,)))
    gate_pre, up_pre = pre[:, :hidden_units], pre[:, hidden_units:]
    sigmoid = 1.0 / (1.0 + jnp.exp(-gate_pre))
    activated = gate_pre * sigmoid
    factor_ref[:, :hidden_units] = up_pre * sigmoid * (1.0 + gate_pre * (1.0 - sigmoid))
    factor_ref[:, hidden_units:] = activated
    hidden = (activated * up_pre).astype(BF)
    half = hidden_units // 2
    unit, at = iota((hidden_units, hidden_units), 0), iota((hidden_units, hidden_units), 1)
    core = jnp.where(at < half, at_ref[1], 1 - at_ref[1])
    share = half // chips
    place = (at & (half - 1)) >> 1
    sign = 1 - 2 * core
    far = jnp.zeros_like(place)
    near = jnp.where(place >= len(NEAR) * len(FAR), 1, 0)
    for move in range(1, len(NEAR)):
        near = near + jnp.where((place >> 2) & 3 == move, NEAR[move], 0)
        far = far + jnp.where(place & 3 == move, FAR[move], 0)
    chip = (at_ref[0] + near * sign + far) & (chips - 1)
    target = (2 * chip + core) * share + (at & 1)
    hidden = dot(hidden, jnp.where(unit == target, 1.0, 0.0).astype(BF), ((1,), (0,))).astype(BF)
    own_ref[...] = hidden[:, :half]
    going = hidden[:, half:]
    tail[...] = got_ref[:, experts_rows(width) :, :].astype(F32)
    for pair in range(width // (2 * LANES)):
        at = slice(pair * 2 * LANES, (pair + 1) * 2 * LANES)
        arrived = read_block(got_ref, tail, pair, experts).astype(BF)
        arrived_ref[:, at] = arrived
        send_ref[:, at] = dot(going, arrived, ((0,), (0,))).astype(BF)


def kept_kernel(own_ref, arrived_ref, out_ref):
    own = own_ref[...]
    for pair in range(out_ref.shape[1] // (2 * LANES)):
        at = slice(pair * 2 * LANES, (pair + 1) * 2 * LANES)
        out_ref[:, at] = dot(own, arrived_ref[:, at], ((0,), (0,)))


def hidden_kernel(arrived_ref, factor_ref, down_ref, out_ref):
    grad_hidden = dot(arrived_ref[...], down_ref[0], ((1,), (1,)))
    out_ref[...] = (jnp.concatenate([grad_hidden, grad_hidden], axis=1) * factor_ref[...]).astype(BF)


def grad_kernel(experts, hidden_ref, gate_ref, up_ref, out_hbm, out_ref, tail, sems):
    hidden = hidden_ref[...]

    def columns(at):
        weight = jnp.concatenate([gate_ref[0, at, :], up_ref[0, at, :]], axis=1)
        return dot(hidden, weight, ((1,), (1,)))

    write_all(columns, gate_ref.shape[1], experts, out_ref, out_hbm, tail, [sems.at[i] for i in range(PARTS)])


def combine_kernel(experts, pick_ref, got_ref, out_ref, tail):
    width = out_ref.shape[1]
    tail[...] = got_ref[:, experts_rows(width) :, :].astype(F32)
    pick = pick_ref[...]
    for pair in range(width // (2 * LANES)):
        rows = read_block(got_ref, tail, pair, experts).astype(BF)
        out_ref[:, pair * 2 * LANES : (pair + 1) * 2 * LANES] = dot(
            pick, rows, ((0,), (0,))
        ).astype(BF)


def fold_kernel(total_ref, *refs):
    *coming, own_ref, first_ref, second_ref, third_ref, lines = refs
    for c in range(lines.shape[1]):
        at = slice(c * LANES, (c + 1) * LANES)
        total = total_ref[:, at]
        for ref in coming:
            total = total + ref[:, at].astype(F32)
        lines[:, c, :] = total
    pieces = lines[...].reshape((len(FAR),) + own_ref.shape)
    own_ref[...] = pieces[0]
    first_ref[...] = pieces[1].astype(BF)
    second_ref[...] = pieces[2].astype(BF)
    third_ref[...] = pieces[3].astype(BF)


def finish_kernel(scale, own_ref, *refs):
    *coming, out_ref, lines = refs
    total = own_ref[...]
    for ref in coming:
        total = total + ref[...].astype(F32)
    lines[...] = (total * scale).reshape(lines.shape)
    for c in range(lines.shape[1]):
        out_ref[0, :, c * LANES : (c + 1) * LANES] = lines[:, c, :]


def per_device(dy_tokens, routing, route_weight, pre_act, gate_weight, up_weight, down_weight):
    experts = lax.axis_size("expert")
    replicas = lax.axis_size("dp")
    tokens, width = dy_tokens.shape
    rows = pre_act.shape[0]
    hidden_units = down_weight.shape[1]
    capacity = rows // experts
    assert capacity == FIRST + 1
    block_rows = capacity * width // LANES
    chips = replicas // 2
    assert chips == 2 * len(NEAR) * len(FAR) and hidden_units == 2 * replicas and FIRST == 8
    shape = jax.ShapeDtypeStruct
    vmem = pl.BlockSpec(memory_space=pltpu.VMEM)
    smem = pl.BlockSpec(memory_space=pltpu.SMEM)
    tail = pltpu.VMEM((experts, width // LANES, LANES), F32)
    block = shape((experts, block_rows, LANES), BF)

    outgoing, pick = pl.pallas_call(
        functools.partial(dispatch_kernel, experts),
        out_shape=(block, shape((rows, tokens), BF)),
        in_specs=[pl.BlockSpec(memory_space=pl.ANY)] * 3,
        out_specs=(vmem, vmem),
        scratch_shapes=[
            pltpu.VMEM((tokens, width), BF),
            pltpu.VMEM(routing.T.shape, jnp.int32),
            pltpu.VMEM(route_weight.T.shape, F32),
            tail,
            pltpu.SemaphoreType.DMA((3,)),
        ],
        compiler_params=PARAMS,
        name="dispatch_rows",
    )(*(pltpu.with_memory_space_constraint(x, pltpu.HBM) for x in (dy_tokens, routing.T, route_weight.T)))
    own = lax.axis_index("dp")
    outgoing, place, pre_act = lax.optimization_barrier(
        (outgoing, jnp.stack([own // 2, own % 2]), pre_act)
    )
    got = lax.all_to_all(outgoing, "expert", split_axis=0, concat_axis=0, tiled=True)

    half = hidden_units // 2
    arrived, own_hidden, send, factor = pl.pallas_call(
        functools.partial(partial_kernel, experts, chips),
        out_shape=(
            shape((rows, width), BF),
            shape((rows, half), BF),
            shape((half, width), BF),
            shape((rows, 2 * hidden_units), F32),
        ),
        in_specs=[smem, vmem, vmem],
        out_specs=(vmem,) * 4,
        scratch_shapes=[tail],
        compiler_params=PARAMS,
        name="down_partial",
    )(place, got, pre_act)
    other = lax.ppermute(send, "dp", [(i, i ^ 1) for i in range(replicas)])
    keep = pl.pallas_call(
        kept_kernel,
        out_shape=shape((half, width), F32),
        in_specs=[vmem] * 2,
        out_specs=vmem,
        compiler_params=PARAMS,
        name="down_kept",
    )(own_hidden, arrived)

    grad_hidden = pl.pallas_call(
        hidden_kernel,
        out_shape=shape((rows, 2 * hidden_units), BF),
        in_specs=[vmem] * 3,
        out_specs=vmem,
        compiler_params=PARAMS,
        name="grad_hidden",
    )(arrived, factor, down_weight)
    other, grad_hidden, keep = lax.optimization_barrier((other, grad_hidden, keep))
    going_back = pl.pallas_call(
        functools.partial(grad_kernel, experts),
        out_shape=pltpu.HBM(block.shape, BF),
        in_specs=[vmem] * 3,
        out_specs=pl.BlockSpec(memory_space=pltpu.HBM),
        scratch_shapes=[
            pltpu.VMEM((experts, block_rows, LANES), BF),
            tail,
            pltpu.SemaphoreType.DMA((PARTS,)),
        ],
        compiler_params=PARAMS,
        name="grad_rows",
    )(grad_hidden, gate_weight, up_weight)
    def pass_on(going, moves):
        hops = [(2 * z + c, 2 * ((z + moves[c]) % chips) + c) for z in range(chips) for c in range(2)]
        return lax.ppermute(going, "dp", hops)

    share = hidden_units // replicas
    count = half // 2
    total = lax.optimization_barrier(keep[:count] + other[:count].astype(F32))
    going = (keep[count:] + other[count:].astype(F32)).astype(BF)
    coming = pass_on(going, (1, -1))
    coming, _ = lax.optimization_barrier((coming, going_back))
    count = count // len(NEAR)
    total, *going = [
        total[at : at + count] + coming[at : at + count].astype(F32)
        for at in range(0, half // 2, count)
    ]
    parts = [pass_on(x.astype(BF), (move, -move)) for x, move in zip(going, NEAR[1:])]
    returned = lax.all_to_all(going_back, "expert", split_axis=0, concat_axis=0, tiled=True)
    piece = (share * width // LANES, LANES)
    own, *going = pl.pallas_call(
        fold_kernel,
        out_shape=(shape(piece, F32),) + (shape(piece, BF),) * 3,
        in_specs=[vmem] * len(NEAR),
        out_specs=(vmem,) * len(FAR),
        scratch_shapes=[pltpu.VMEM((count, width // LANES, LANES), F32)],
        compiler_params=PARAMS,
        name="fold",
    )(total, *parts)
    parts = [pass_on(x, (move, move)) for x, move in zip(going, FAR[1:])]
    grad_tokens = pl.pallas_call(
        functools.partial(combine_kernel, experts),
        out_shape=shape((tokens, width), BF),
        in_specs=[vmem] * 2,
        out_specs=vmem,
        scratch_shapes=[tail],
        compiler_params=PARAMS,
        name="combine_rows",
    )(pick, returned)
    parts[0], grad_tokens = lax.optimization_barrier((parts[0], grad_tokens))
    grad_down = pl.pallas_call(
        functools.partial(finish_kernel, 1.0 / replicas),
        out_shape=shape((1, share, width), F32),
        in_specs=[vmem] * len(FAR),
        out_specs=vmem,
        scratch_shapes=[pltpu.VMEM((share, width // LANES, LANES), F32)],
        compiler_params=PARAMS,
        name="finish",
    )(own, *parts)
    return (grad_tokens, grad_down)


def solution(mesh):
    placed = (
        P(("dp", "expert"), None),
        P(("dp", "expert"), None),
        P(("dp", "expert"), None),
        P(("dp", "expert"), None),
        P("expert", None, None),
        P("expert", None, None),
        P("expert", None, None),
    )
    return jax.shard_map(
        per_device,
        mesh=mesh,
        in_specs=placed,
        out_specs=(P(("dp", "expert"), None), P("expert", "dp", None)),
        check_vma=False,
    )
```

```python
import functools

import jax
import jax.numpy as jnp
from jax import lax
from jax.experimental import pallas as pl
from jax.experimental.pallas import tpu as pltpu
from jax.sharding import PartitionSpec as P

BF = jnp.bfloat16
F32 = jnp.float32
LANES = 128
FIRST = 8
NEAR = (0, -2, 2, -4)
FAR = (0, 16, -8, 8)
PARAMS = pltpu.CompilerParams(vmem_limit_bytes=16 * 1024 * 1024)


def dot(a, b, contract):
    return lax.dot_general(a, b, (contract, ((), ())), preferred_element_type=F32)


def iota(shape, axis):
    return lax.broadcasted_iota(jnp.int32, shape, axis)


def write_block(ref, tail, pair, first, second, experts):
    main = experts * FIRST
    tiles = [x[:main].reshape(experts, FIRST, LANES) for x in (first, second)]
    ref[:, pair * 16 : pair * 16 + 16, :] = jnp.concatenate(tiles, axis=1).astype(BF)
    tail[:, 2 * pair, :] = first[main:]
    tail[:, 2 * pair + 1, :] = second[main:]


def read_block(ref, tail, pair, experts):
    both = ref[:, pair * 16 : pair * 16 + 16, :].astype(F32)
    main = experts * FIRST
    halves = []
    for at in range(2):
        block = both[:, at * FIRST : (at + 1) * FIRST, :].reshape(main, LANES)
        halves.append(jnp.concatenate([block, tail[:, 2 * pair + at, :]], axis=0))
    return jnp.concatenate(halves, axis=1)


def dispatch_kernel(
    experts, dy_hbm, routing_hbm, weight_hbm, out_ref, pick_ref, dy_ref, routing_ref, weight_ref, tail, sems
):
    loads = [
        pltpu.make_async_copy(source, target, sems.at[i])
        for i, (source, target) in enumerate(
            [(routing_hbm, routing_ref), (weight_hbm, weight_ref), (dy_hbm, dy_ref)]
        )
    ]
    for load in loads:
        load.start()
    loads[0].wait()
    loads[1].wait()
    tokens, width = dy_ref.shape
    route_count = routing_ref.shape[0]
    main = experts * FIRST
    rows = main + experts
    slot = iota((rows, tokens), 0)
    expert = jnp.where(slot < main, slot >> 3, slot - main)
    position = jnp.where(slot < main, slot & (FIRST - 1), FIRST)
    named = jnp.zeros((rows, tokens), F32)
    scale = jnp.zeros((rows, tokens), F32)
    for k in range(route_count):
        hit = routing_ref[k : k + 1, :] == expert
        named = named + jnp.where(hit, 1.0, 0.0)
        scale = scale + jnp.where(hit, weight_ref[k : k + 1, :], 0.0)
    earlier = jnp.where(iota((tokens, tokens), 0) < iota((tokens, tokens), 1), 1.0, 0.0)
    before = dot(named.astype(BF), earlier.astype(BF), ((1,), (0,)))
    pick = jnp.where((named > 0.5) & (before == position.astype(F32)), 1.0, 0.0)
    chosen = pick.astype(BF)
    pick_ref[...] = chosen
    row_weight = jnp.sum(pick * scale, axis=1, keepdims=True)
    loads[2].wait()

    for pair in range(width // (2 * LANES)):
        at = slice(pair * 2 * LANES, (pair + 1) * 2 * LANES)
        part = dot(chosen, dy_ref[:, at], ((1,), (0,))) * row_weight
        write_block(out_ref, tail, pair, part[:, :LANES], part[:, LANES:], experts)
    out_ref[:, experts_rows(width) :, :] = tail[...].astype(BF)


def write_all(columns, width, experts, out_ref, tail):
    for pair in range(width // (2 * LANES)):
        part = columns(slice(pair * 2 * LANES, (pair + 1) * 2 * LANES))
        write_block(out_ref, tail, pair, part[:, :LANES], part[:, LANES:], experts)
    out_ref[:, experts_rows(width) :, :] = tail[...].astype(BF)


def experts_rows(width):
    return width // LANES * FIRST


def partial_kernel(
    experts, chips, at_ref, got_ref, pre_ref, arrived_ref, own_ref, send_ref, factor_ref, tail
):
    rows, width = arrived_ref.shape
    hidden_units = pre_ref.shape[1] // 2
    main = experts * FIRST
    capacity = rows // experts
    new, old = iota((rows, rows), 0), iota((rows, rows), 1)
    source = jnp.where(
        new < main, (new >> 3) * capacity + (new & (FIRST - 1)), (new - main) * capacity + FIRST
    )
    order = jnp.where(source == old, 1.0, 0.0).astype(BF)
    pre = dot(order, pre_ref[...], ((1,), (0,)))
    gate_pre, up_pre = pre[:, :hidden_units], pre[:, hidden_units:]
    sigmoid = 1.0 / (1.0 + jnp.exp(-gate_pre))
    activated = gate_pre * sigmoid
    factor_ref[:, :hidden_units] = up_pre * sigmoid * (1.0 + gate_pre * (1.0 - sigmoid))
    factor_ref[:, hidden_units:] = activated
    hidden = (activated * up_pre).astype(BF)
    half = hidden_units // 2
    unit, at = iota((hidden_units, hidden_units), 0), iota((hidden_units, hidden_units), 1)
    core = jnp.where(at < half, at_ref[1], 1 - at_ref[1])
    share = half // chips
    place = (at & (half - 1)) >> 1
    sign = 1 - 2 * core
    far = jnp.zeros_like(place)
    near = jnp.where(place >= len(NEAR) * len(FAR), 1, 0)
    for move in range(1, len(NEAR)):
        near = near + jnp.where((place >> 2) & 3 == move, NEAR[move], 0)
        far = far + jnp.where(place & 3 == move, FAR[move], 0)
    chip = (at_ref[0] + near * sign + far) & (chips - 1)
    target = (2 * chip + core) * share + (at & 1)
    hidden = dot(hidden, jnp.where(unit == target, 1.0, 0.0).astype(BF), ((1,), (0,))).astype(BF)
    own_ref[...] = hidden[:, :half]
    going = hidden[:, half:]
    tail[...] = got_ref[:, experts_rows(width) :, :].astype(F32)
    for pair in range(width // (2 * LANES)):
        at = slice(pair * 2 * LANES, (pair + 1) * 2 * LANES)
        arrived = read_block(got_ref, tail, pair, experts).astype(BF)
        arrived_ref[:, at] = arrived
        send_ref[:, at] = dot(going, arrived, ((0,), (0,))).astype(BF)


def kept_kernel(own_ref, arrived_ref, out_ref):
    own = own_ref[...]
    for pair in range(out_ref.shape[1] // (2 * LANES)):
        at = slice(pair * 2 * LANES, (pair + 1) * 2 * LANES)
        out_ref[:, at] = dot(own, arrived_ref[:, at], ((0,), (0,)))


def hidden_kernel(arrived_ref, factor_ref, down_ref, out_ref):
    grad_hidden = dot(arrived_ref[...], down_ref[0], ((1,), (1,)))
    out_ref[...] = (jnp.concatenate([grad_hidden, grad_hidden], axis=1) * factor_ref[...]).astype(BF)


def grad_kernel(experts, hidden_ref, gate_ref, up_ref, out_hbm, out_ref, tail, sem):
    hidden = hidden_ref[...]

    def columns(at):
        weight = jnp.concatenate([gate_ref[0, at, :], up_ref[0, at, :]], axis=1)
        return dot(hidden, weight, ((1,), (1,)))

    write_all(columns, gate_ref.shape[1], experts, out_ref, tail)
    store = pltpu.make_async_copy(out_ref, out_hbm, sem)
    store.start()
    store.wait()


def combine_kernel(experts, pick_ref, got_ref, out_ref, tail):
    width = out_ref.shape[1]
    tail[...] = got_ref[:, experts_rows(width) :, :].astype(F32)
    pick = pick_ref[...]
    for pair in range(width // (2 * LANES)):
        rows = read_block(got_ref, tail, pair, experts).astype(BF)
        out_ref[:, pair * 2 * LANES : (pair + 1) * 2 * LANES] = dot(
            pick, rows, ((0,), (0,))
        ).astype(BF)


def fold_kernel(total_ref, *refs):
    *coming, own_ref, first_ref, second_ref, third_ref, lines = refs
    for c in range(lines.shape[1]):
        at = slice(c * LANES, (c + 1) * LANES)
        total = total_ref[:, at]
        for ref in coming:
            total = total + ref[:, at].astype(F32)
        lines[:, c, :] = total
    pieces = lines[...].reshape((len(FAR),) + own_ref.shape)
    own_ref[...] = pieces[0]
    first_ref[...] = pieces[1].astype(BF)
    second_ref[...] = pieces[2].astype(BF)
    third_ref[...] = pieces[3].astype(BF)


def finish_kernel(scale, own_ref, *refs):
    *coming, out_ref, lines = refs
    total = own_ref[...]
    for ref in coming:
        total = total + ref[...].astype(F32)
    lines[...] = (total * scale).reshape(lines.shape)
    for c in range(lines.shape[1]):
        out_ref[0, :, c * LANES : (c + 1) * LANES] = lines[:, c, :]


def per_device(dy_tokens, routing, route_weight, pre_act, gate_weight, up_weight, down_weight):
    experts = lax.axis_size("expert")
    replicas = lax.axis_size("dp")
    tokens, width = dy_tokens.shape
    rows = pre_act.shape[0]
    hidden_units = down_weight.shape[1]
    capacity = rows // experts
    assert capacity == FIRST + 1
    block_rows = capacity * width // LANES
    chips = replicas // 2
    assert chips == 2 * len(NEAR) * len(FAR) and hidden_units == 2 * replicas and FIRST == 8
    shape = jax.ShapeDtypeStruct
    vmem = pl.BlockSpec(memory_space=pltpu.VMEM)
    smem = pl.BlockSpec(memory_space=pltpu.SMEM)
    tail = pltpu.VMEM((experts, width // LANES, LANES), F32)
    block = shape((experts, block_rows, LANES), BF)

    outgoing, pick = pl.pallas_call(
        functools.partial(dispatch_kernel, experts),
        out_shape=(block, shape((rows, tokens), BF)),
        in_specs=[pl.BlockSpec(memory_space=pl.ANY)] * 3,
        out_specs=(vmem, vmem),
        scratch_shapes=[
            pltpu.VMEM((tokens, width), BF),
            pltpu.VMEM(routing.T.shape, jnp.int32),
            pltpu.VMEM(route_weight.T.shape, F32),
            tail,
            pltpu.SemaphoreType.DMA((3,)),
        ],
        compiler_params=PARAMS,
        name="dispatch_rows",
    )(*(pltpu.with_memory_space_constraint(x, pltpu.HBM) for x in (dy_tokens, routing.T, route_weight.T)))
    own = lax.axis_index("dp")
    outgoing, place, pre_act = lax.optimization_barrier(
        (outgoing, jnp.stack([own // 2, own % 2]), pre_act)
    )
    got = lax.all_to_all(outgoing, "expert", split_axis=0, concat_axis=0, tiled=True)

    half = hidden_units // 2
    arrived, own_hidden, send, factor = pl.pallas_call(
        functools.partial(partial_kernel, experts, chips),
        out_shape=(
            shape((rows, width), BF),
            shape((rows, half), BF),
            shape((half, width), BF),
            shape((rows, 2 * hidden_units), F32),
        ),
        in_specs=[smem, vmem, vmem],
        out_specs=(vmem,) * 4,
        scratch_shapes=[tail],
        compiler_params=PARAMS,
        name="down_partial",
    )(place, got, pre_act)
    other = lax.ppermute(send, "dp", [(i, i ^ 1) for i in range(replicas)])
    keep = pl.pallas_call(
        kept_kernel,
        out_shape=shape((half, width), F32),
        in_specs=[vmem] * 2,
        out_specs=vmem,
        compiler_params=PARAMS,
        name="down_kept",
    )(own_hidden, arrived)

    grad_hidden = pl.pallas_call(
        hidden_kernel,
        out_shape=shape((rows, 2 * hidden_units), BF),
        in_specs=[vmem] * 3,
        out_specs=vmem,
        compiler_params=PARAMS,
        name="grad_hidden",
    )(arrived, factor, down_weight)
    other, grad_hidden, keep = lax.optimization_barrier((other, grad_hidden, keep))
    going_back = pl.pallas_call(
        functools.partial(grad_kernel, experts),
        out_shape=pltpu.HBM(block.shape, BF),
        in_specs=[vmem] * 3,
        out_specs=pl.BlockSpec(memory_space=pltpu.HBM),
        scratch_shapes=[
            pltpu.VMEM((experts, block_rows, LANES), BF),
            tail,
            pltpu.SemaphoreType.DMA,
        ],
        compiler_params=PARAMS,
        name="grad_rows",
    )(grad_hidden, gate_weight, up_weight)
    def pass_on(going, moves):
        hops = [(2 * z + c, 2 * ((z + moves[c]) % chips) + c) for z in range(chips) for c in range(2)]
        return lax.ppermute(going, "dp", hops)

    share = hidden_units // replicas
    count = half // 2
    total = lax.optimization_barrier(keep[:count] + other[:count].astype(F32))
    going = (keep[count:] + other[count:].astype(F32)).astype(BF)
    coming = pass_on(going, (1, -1))
    coming, _ = lax.optimization_barrier((coming, going_back))
    count = count // len(NEAR)
    total, *going = [
        total[at : at + count] + coming[at : at + count].astype(F32)
        for at in range(0, half // 2, count)
    ]
    parts = [pass_on(x.astype(BF), (move, -move)) for x, move in zip(going, NEAR[1:])]
    returned = lax.all_to_all(going_back, "expert", split_axis=0, concat_axis=0, tiled=True)
    piece = (share * width // LANES, LANES)
    own, *going = pl.pallas_call(
        fold_kernel,
        out_shape=(shape(piece, F32),) + (shape(piece, BF),) * 3,
        in_specs=[vmem] * len(NEAR),
        out_specs=(vmem,) * len(FAR),
        scratch_shapes=[pltpu.VMEM((count, width // LANES, LANES), F32)],
        compiler_params=PARAMS,
        name="fold",
    )(total, *parts)
    parts = [pass_on(x, (move, move)) for x, move in zip(going, FAR[1:])]
    grad_tokens = pl.pallas_call(
        functools.partial(combine_kernel, experts),
        out_shape=shape((tokens, width), BF),
        in_specs=[vmem] * 2,
        out_specs=vmem,
        scratch_shapes=[tail],
        compiler_params=PARAMS,
        name="combine_rows",
    )(pick, returned)
    parts[0], grad_tokens = lax.optimization_barrier((parts[0], grad_tokens))
    grad_down = pl.pallas_call(
        functools.partial(finish_kernel, 1.0 / replicas),
        out_shape=shape((1, share, width), F32),
        in_specs=[vmem] * len(FAR),
        out_specs=vmem,
        scratch_shapes=[pltpu.VMEM((share, width // LANES, LANES), F32)],
        compiler_params=PARAMS,
        name="finish",
    )(own, *parts)
    return (grad_tokens, grad_down)


def solution(mesh):
    placed = (
        P(("dp", "expert"), None),
        P(("dp", "expert"), None),
        P(("dp", "expert"), None),
        P(("dp", "expert"), None),
        P("expert", None, None),
        P("expert", None, None),
        P("expert", None, None),
    )
    return jax.shard_map(
        per_device,
        mesh=mesh,
        in_specs=placed,
        out_specs=(P(("dp", "expert"), None), P("expert", "dp", None)),
        check_vma=False,
    )
```
